512 devices in a mesh: sec: 128 (over y, z, core), op: 4 (over x).
Axes of the slice: x: 4, y: 8, z: 8, core: 2. Of those that a mesh axis runs over, the one named last changes fastest.
Arguments:
- trial_state: bfloat16 [2, 8192, 8192], P(None, 'sec'), may hold values from -6 to 6
- left_operators: bfloat16 [24, 8192, 64], P('op', 'sec'), may hold values from -0.75 to 0.75
- right_operators: bfloat16 [24, 8192, 64], P('op', 'sec'), may hold values from -0.15625 to 0.15625
- left_coupling: int32 [24, 128], P('op', 'sec'), may hold values from -2 to 2
- right_coupling: int32 [24, 128], P('op', 'sec'), may hold values from -2 to 2
- left_charge: int32 [128], replicated, may hold values from 0 to 6
- right_charge: int32 [128], replicated, may hold values from 0 to 6
Outputs:
- sigma_columns: bfloat16 [2, 8192, 8192], P(None, 'sec', 'op')
The draws below stay inside these ranges and needn't reach their ends.
All inputs are finite; a program needn't handle non-finite values.
Results may differ from the reference program's by a relative error of at most 0.0049.
Values may be sent and summed in bfloat16 or wider, within the bound.
No kernel may reach another device: no remote copies, remote signals or barrier semaphores. Data moves between devices by JAX's collectives and lax.ppermute only.
A program may use at most 128 MiB of HBM per device.

```python
import jax
import jax.numpy as jnp
from jax import lax

BLOCK = 64
TERMS = 24
NVEC = 2
SECTORS = 128
STATES = 8192


def touch_ends(drawn, rng, least, top_value):
    place = [jax.random.randint(jax.random.fold_in(rng, axis), (), 0, length) for axis, length in enumerate(drawn.shape)]
    widest = drawn.shape.index(max(drawn.shape))
    beside = place[:widest] + [(place[widest] + 1) % drawn.shape[widest]] + place[widest + 1:]
    return drawn.at[tuple(place)].set(least).at[tuple(beside)].set(top_value)


def shard_levels(own_key, shape, cuts, low, top_value):
    gain = 1.0
    for axis_at, shards_of in cuts:
        draws = jax.random.uniform(jax.random.fold_in(jax.random.fold_in(own_key, 6), axis_at), (shards_of,), jnp.float32, low / len(cuts), top_value / len(cuts))
        gain = gain * jnp.repeat(jnp.exp(draws), shape[axis_at] // shards_of).reshape((-1,) + (1,) * (len(shape) - 1 - axis_at))
    return gain


def scatter_about(key, shape, scale, bound, cuts=(), kind=jnp.bfloat16):
    drawn = jax.random.normal(key, shape, jnp.float32) * scale
    if len(cuts) > 0:
        drawn = shard_levels(key, shape, cuts, -0.22, 0.18) * drawn
    return jnp.clip(drawn, min=-bound, max=bound).astype(kind)


def setup_inputs(seed: int = 0) -> dict:
    streams_of = jax.random.split(jax.random.key(seed), 8)
    trial_state = scatter_about(streams_of[0], (NVEC, STATES, STATES), 1.0, 6.0, ((1, 128),))
    left_operators = scatter_about(streams_of[1], (TERMS, STATES, BLOCK), BLOCK ** -0.5, 0.75, ((0, 4), (1, 128)))
    right_operators = scatter_about(streams_of[2], (TERMS, STATES, BLOCK), (BLOCK * TERMS) ** -0.5, 0.15625, ((0, 4), (1, 128)))
    left_coupling = touch_ends(jax.random.randint(streams_of[3], (TERMS, SECTORS), -2, 3), jax.random.fold_in(streams_of[3], 1), -2, 2).astype(jnp.int32)
    right_coupling = touch_ends(jax.random.randint(streams_of[4], (TERMS, SECTORS), -2, 3), jax.random.fold_in(streams_of[4], 1), -2, 2).astype(jnp.int32)
    left_charge = touch_ends(jax.random.randint(streams_of[5], (SECTORS,), 0, 7), jax.random.fold_in(streams_of[5], 1), 0, 6).astype(jnp.int32)
    right_charge = touch_ends(jax.random.randint(streams_of[6], (SECTORS,), 0, 7), jax.random.fold_in(streams_of[6], 1), 0, 6).astype(jnp.int32)
    return dict(trial_state=trial_state, left_operators=left_operators, right_operators=right_operators, left_coupling=left_coupling, right_coupling=right_coupling, left_charge=left_charge, right_charge=right_charge)


target_charge = 6


def reference(trial_state, left_operators, right_operators, left_coupling, right_coupling, left_charge, right_charge):
    allowed = (jnp.abs(left_charge[:, None] + right_charge[None, :] - target_charge) <= 1).astype(jnp.float32)
    full_mask = jnp.repeat(jnp.repeat(allowed, BLOCK, axis=0), BLOCK, axis=1)
    masked = (trial_state.astype(jnp.float32) * full_mask[None]).astype(jnp.bfloat16)
    state_five = masked.astype(jnp.float32).reshape(NVEC, SECTORS, BLOCK, SECTORS, BLOCK)

    def add_term(total, pieces):
        left_op, right_op, left_c, right_c = pieces
        left_b = left_op.astype(jnp.float32).reshape(SECTORS, BLOCK, BLOCK) * left_c.astype(jnp.float32)[:, None, None]
        products = jnp.einsum("aik,vakbj->vbjai", left_b, state_five).astype(jnp.bfloat16)
        right_b = right_op.astype(jnp.float32).reshape(SECTORS, BLOCK, BLOCK) * right_c.astype(jnp.float32)[:, None, None]
        return total + jnp.einsum("bjk,vbkai->vbjai", right_b, products.astype(jnp.float32)), None

    start = jnp.zeros((NVEC, SECTORS, BLOCK, SECTORS, BLOCK), jnp.float32)
    total, unused = lax.scan(add_term, start, (left_operators, right_operators, left_coupling, right_coupling))
    result = total.reshape(NVEC, STATES, STATES) * full_mask.T[None]
    return result.astype(jnp.bfloat16)
```

```python
import jax
import jax.numpy as jnp
import numpy as np
from jax import lax
from jax.experimental import pallas as pl
from jax.experimental.pallas import tpu as pltpu
from jax.sharding import Mesh, PartitionSpec as P

target_charge = 6
XDIM, YH, YL, ZH, ZL, CORE = 4, 4, 2, 4, 2, 2
SEC = ("yh", "yl", "zh", "zl", "core")
FAR = ("yh", "yl", "zh")
NEAR = ("zl", "core")
NT = (((1,), (1,)), ((), ()))
VMEM = 48 * 1024 * 1024


def same_block(rows, lanes, block):
    row = lax.broadcasted_iota(jnp.int32, (rows, lanes), 0) // block
    lane = lax.broadcasted_iota(jnp.int32, (rows, lanes), 1) // block
    return row == lane


def block_diagonal(piece, mask):
    copies = mask.shape[0] // piece.shape[0]
    stacked = jnp.concatenate([piece] * copies, axis=0)
    return jnp.where(mask, stacked, jnp.zeros_like(stacked))


def right_kernel(block, terms, recv_ref, half_ref):
    v, g = pl.program_id(0), pl.program_id(1)
    half = block // 2
    group = 4 * block
    rows = []
    for a in range(4):
        for h in range(2):
            start = pl.multiple_of((g * 4 + a) * half, half)
            rows.append(recv_ref[v * 2 + h, pl.ds(start, half), :])
    state = jnp.concatenate(rows, axis=0)
    mask = same_block(group, group, block)
    per = terms // XDIM
    for t in range(terms):
        at = 8 * half + (t % per) * block
        right = block_diagonal(recv_ref[t // per, at:at + block, :], mask)
        out = lax.dot_general(right, state, NT, preferred_element_type=jnp.float32)
        half_ref[0, 0, :, t * group:(t + 1) * group] = out.astype(half_ref.dtype)


def left_kernel(block, terms, half_ref, left_ref, out_ref, diag_ref):
    group = 4 * block
    per = terms // XDIM

    @pl.when(pl.program_id(1) == 0)
    def _():
        mask = same_block(group, group, block)
        for t in range(terms):
            at = (t % per) * block
            diag_ref[:, t * group:(t + 1) * group] = block_diagonal(
                left_ref[t // per, 0, at:at + block, :], mask
            )

    out = lax.dot_general(half_ref[0, 0], diag_ref[...], NT, preferred_element_type=jnp.float32)
    out_ref[...] = out.reshape(4, 1, block, group).astype(out_ref.dtype)


def merge_kernel(block, in_ref, out_ref):
    wide = 2 * block
    for m in range(in_ref.shape[3] // wide):
        for s in range(2):
            low = in_ref[2 * s, 0, :, m * wide:(m + 1) * wide]
            high = in_ref[2 * s + 1, 0, :, m * wide:(m + 1) * wide]
            even = jnp.concatenate([low[:, :block], high[:, :block]], axis=1)
            odd = jnp.concatenate([low[:, block:], high[:, block:]], axis=1)
            at = (2 * m * 2 + s) * wide
            out_ref[0, :, at:at + wide] = even
            at = ((2 * m + 1) * 2 + s) * wide
            out_ref[0, :, at:at + wide] = odd


def body(
    trial_state,
    left_operators,
    right_operators,
    left_coupling,
    right_coupling,
    left_charge,
    right_charge,
):
    vectors, block, states = trial_state.shape
    here = left_operators.shape[0]
    terms = here * XDIM
    group = 4 * block
    half = block // 2
    plane = lax.axis_index("op")
    position = lax.axis_index(SEC)

    left = left_operators * left_coupling[:, :, None].astype(jnp.bfloat16)
    left = left.reshape(here // 2, 2, block, block).transpose(0, 2, 1, 3)
    left = left.reshape(here // 2 * block, 2 * block)
    swap = [(q * XDIM + x, x * XDIM + q) for q in range(YH) for x in range(XDIM)]
    left = lax.ppermute(left, ("yh", "op"), swap)
    left = jnp.broadcast_to(left[None], (ZH,) + left.shape)
    left = lax.all_to_all(left, "zh", 0, 0, tiled=True)
    left = left.reshape(ZH, here // 2, block, 2, block).transpose(1, 3, 2, 0, 4)
    left = left.reshape(here * block, group)
    left = lax.all_gather(left, ("yh", "yl"), tiled=True)
    left = left.reshape(YH, YL, here * block, group)

    right = right_operators * right_coupling[:, :, None].astype(jnp.bfloat16)
    other = lax.ppermute(right, "core", [(0, 1), (1, 0)])
    first = lax.axis_index("core") == 0
    right = jnp.concatenate(
        [jnp.where(first, right, other), jnp.where(first, other, right)], axis=2
    ).reshape(here * block, 2 * block)
    other = lax.ppermute(right, "zl", [(0, 1), (1, 0)])
    first = lax.axis_index("zl") == 0
    right = jnp.concatenate(
        [jnp.where(first, right, other), jnp.where(first, other, right)], axis=1
    )

    own = lax.dynamic_slice_in_dim(left_charge, position, 1)
    allowed = (jnp.abs(own + right_charge - target_charge) <= 1).astype(jnp.bfloat16)
    quarter = lax.dynamic_slice(
        trial_state, (plane // 2, (plane % 2) * half, 0), (1, half, states)
    )[0]
    quarter = quarter * jnp.repeat(allowed, block)[None, :]
    quarter = quarter.reshape(half, states // group, group).transpose(1, 0, 2)
    quarter = lax.all_to_all(quarter, FAR, 0, 0, tiled=True)
    quarter = quarter.reshape(YH, YL * ZH * half, group)
    packed = jnp.concatenate(
        [quarter, jnp.broadcast_to(right[None], (XDIM,) + right.shape)], axis=1
    )
    packed = lax.all_to_all(packed, "op", 0, 0, tiled=True)

    half_done = pl.pallas_call(
        lambda *refs: right_kernel(block, terms, *refs),
        grid=(vectors, YL),
        in_specs=[pl.BlockSpec(packed.shape, lambda v, g: (0, 0, 0))],
        out_specs=pl.BlockSpec((1, 1, group, terms * group), lambda v, g: (v, g, 0, 0)),
        out_shape=jax.ShapeDtypeStruct((vectors, YL, group, terms * group), jnp.bfloat16),
        compiler_params=pltpu.CompilerParams(vmem_limit_bytes=VMEM),
        name="right_products",
    )(packed)

    partial = pl.pallas_call(
        lambda *refs: left_kernel(block, terms, *refs),
        grid=(YL, vectors),
        in_specs=[
            pl.BlockSpec((1, 1, group, terms * group), lambda g, v: (v, g, 0, 0)),
            pl.BlockSpec((YH, 1, here * block, group), lambda g, v: (0, g, 0, 0)),
        ],
        out_specs=pl.BlockSpec((4, 1, block, group), lambda g, v: (0, v, 0, g)),
        out_shape=jax.ShapeDtypeStruct((4, vectors, block, YL * group), jnp.bfloat16),
        scratch_shapes=[pltpu.VMEM((group, terms * group), jnp.bfloat16)],
        compiler_params=pltpu.CompilerParams(vmem_limit_bytes=VMEM),
        name="left_products",
    )(half_done, left)

    partial = lax.all_to_all(partial, NEAR, 0, 0, tiled=True)
    return pl.pallas_call(
        lambda *refs: merge_kernel(block, *refs),
        grid=(vectors,),
        in_specs=[pl.BlockSpec((4, 1, block, YL * group), lambda v: (0, v, 0, 0))],
        out_specs=pl.BlockSpec((1, block, 4 * YL * group), lambda v: (v, 0, 0)),
        out_shape=jax.ShapeDtypeStruct((vectors, block, 4 * YL * group), jnp.bfloat16),
        name="merge_sectors",
    )(partial)


def solution(mesh):
    fine = Mesh(mesh.devices.reshape(YH, YL, ZH, ZL, CORE, XDIM), SEC + ("op",))
    return jax.shard_map(
        body,
        mesh=fine,
        in_specs=(
            P(None, SEC, None),
            P("op", SEC, None),
            P("op", SEC, None),
            P("op", SEC),
            P("op", SEC),
            P(),
            P(),
        ),
        out_specs=P(None, SEC, "op"),
        check_vma=False,
    )
```

```python
import jax
import jax.numpy as jnp
from jax import lax
from jax.experimental import pallas as pl
from jax.experimental.pallas import tpu as pltpu
from jax.sharding import Mesh, PartitionSpec as P

target_charge = 6
XDIM, YH, YL, ZH, ZL, CORE = 4, 4, 2, 4, 2, 2
SEC = ("yh", "yl", "zh", "zl", "core")
FAR = ("yh", "zh", "core")
NEAR = ("yl", "zl")
NT = (((1,), (1,)), ((), ()))
BLOCK = 64
WIDE = 2 * BLOCK
HALF = BLOCK // 2
GROUP = 4 * BLOCK
TERMS = 24
HERE = TERMS // XDIM
PAIRS = HERE // 2
XROWS = 2 * HALF
LROWS = PAIRS * HALF
RROWS = PAIRS * BLOCK
FROM = ZH * CORE
VMEM = 48 * 1024 * 1024


def swap_halves(piece):
    return jnp.concatenate([piece[:, BLOCK:], piece[:, :BLOCK]], axis=1)


def placed(piece, second, to_second):
    lane = lax.broadcasted_iota(jnp.int32, piece.shape, 1)
    moved = piece if second == to_second else swap_halves(piece)
    keep = (lane >= BLOCK) if to_second else (lane < BLOCK)
    return jnp.where(keep, moved, jnp.zeros_like(moved))


def pack_kernel(lc_ref, rc_ref, left_ref, right_ref, lout_ref, rout_ref):
    for p in range(PAIRS):
        left, right = [], []
        for t in (2 * p, 2 * p + 1):
            scale = lc_ref[t, 0].astype(jnp.float32)
            left.append((left_ref[t].astype(jnp.float32) * scale).astype(jnp.bfloat16))
            scale = rc_ref[t, 0].astype(jnp.float32)
            right.append((right_ref[t].astype(jnp.float32) * scale).astype(jnp.bfloat16))
        rout_ref[p * BLOCK:(p + 1) * BLOCK, :] = jnp.concatenate(right, axis=1)
        both = jnp.concatenate(left, axis=1)
        for h in range(2):
            lout_ref[h, p * HALF:(p + 1) * HALF, :] = both[h * HALF:(h + 1) * HALF]


def send_kernel(at_ref, lcharge_ref, rcharge_ref, x_ref, out_ref):
    own = lcharge_ref[at_ref[2]] - target_charge
    lane = lax.broadcasted_iota(jnp.int32, (1, WIDE), 1)

    def allowed(sector):
        return jnp.where(jnp.abs(own + rcharge_ref[sector]) <= 1, 1.0, 0.0)

    for yh in range(YH):
        for yl in range(YL):
            for zh in range(ZH):
                at = ((yh * YL + yl) * ZH + zh) * ZL
                first = x_ref[0, :, at * WIDE:(at + 1) * WIDE]
                second = x_ref[0, :, (at + 1) * WIDE:(at + 2) * WIDE]
                for c in range(CORE):
                    lanes = slice(c * BLOCK, (c + 1) * BLOCK)
                    both = jnp.concatenate([first[:, lanes], second[:, lanes]], axis=1)
                    mask = jnp.where(
                        lane < BLOCK, allowed(at * CORE + c), allowed((at + 1) * CORE + c)
                    ).astype(jnp.bfloat16)
                    to = (yh * ZH + zh) * CORE + c
                    out_ref[to, yl * HALF:(yl + 1) * HALF, :] = both * mask


def sigma_kernel(core_ref, xr_ref, own_ref, other_ref, out_ref, right_ref, left_ref, half_ref):
    g, v = pl.program_id(0), pl.program_id(1)
    core = core_ref[0]

    @pl.when((g == 0) & (v == 0))
    def _():
        right_ref[...] = jnp.zeros_like(right_ref)
        left_ref[...] = jnp.zeros_like(left_ref)
        for x in range(XDIM):
            for p in range(PAIRS):
                for b in range(4):
                    at = FROM * XROWS + b * RROWS + p * BLOCK
                    piece = xr_ref[x, at:at + BLOCK, :]
                    for s in range(2):
                        t = x * HERE + 2 * p + s
                        right_ref[t, b * BLOCK:(b + 1) * BLOCK,
                                  (b // 2) * WIDE:(b // 2 + 1) * WIDE] = placed(piece, s, b % 2)

    @pl.when(v == 0)
    def _():
        for x in range(XDIM):
            for p in range(PAIRS):
                for a in range(4):
                    for ref, h in ((own_ref, core), (other_ref, 1 - core)):
                        piece = ref[x * FROM + g * 4 + a, p * HALF:(p + 1) * HALF, :]
                        rows = pl.ds(pl.multiple_of(a * BLOCK + h * HALF, HALF), HALF)
                        for s in range(2):
                            t = x * HERE + 2 * p + s
                            at = t * GROUP + (a // 2) * WIDE
                            left_ref[rows, at:at + WIDE] = placed(piece, s, a % 2)

    rows = []
    for a in range(4):
        for h in range(2):
            start = pl.multiple_of((g * 4 + a) * XROWS, XROWS)
            piece = xr_ref[v * 2 + h, pl.ds(start, XROWS), :]
            rows.append(jnp.concatenate([piece[:HALF], piece[HALF:]], axis=1))
    state = jnp.concatenate(rows, axis=0)
    for t in range(TERMS):
        out = lax.dot_general(right_ref[t], state, NT, preferred_element_type=jnp.float32)
        half_ref[:, t * GROUP:(t + 1) * GROUP] = out.astype(half_ref.dtype)
    out = lax.dot_general(half_ref[...], left_ref[...], NT, preferred_element_type=jnp.float32)
    out_ref[...] = out.reshape(4, 1, BLOCK, GROUP).astype(out_ref.dtype)


def merge_kernel(in_ref, out_ref):
    for yl in range(YL):
        for zh in range(ZH):
            for zl in range(ZL):
                at = ((yl * ZH + zh) * ZL + zl) * WIDE
                out_ref[0, :, at:at + WIDE] = in_ref[yl * ZL + zl, 0, :, zh * WIDE:(zh + 1) * WIDE]


def body(
    trial_state,
    left_operators,
    right_operators,
    left_coupling,
    right_coupling,
    left_charge,
    right_charge,
):
    vectors, _, states = trial_state.shape
    plane = lax.axis_index("op")
    position = lax.axis_index(SEC)
    smem = pl.BlockSpec(memory_space=pltpu.SMEM)
    vmem = pl.BlockSpec(memory_space=pltpu.VMEM)
    params = pltpu.CompilerParams(vmem_limit_bytes=VMEM)

    left, right = pl.pallas_call(
        pack_kernel,
        in_specs=[smem, smem, vmem, vmem],
        out_specs=[vmem, vmem],
        out_shape=[
            jax.ShapeDtypeStruct((2, LROWS, WIDE), jnp.bfloat16),
            jax.ShapeDtypeStruct((RROWS, WIDE), jnp.bfloat16),
        ],
        name="pack_operators",
    )(left_coupling, right_coupling, left_operators, right_operators)
    swap = [(q * XDIM + x, x * XDIM + q) for q in range(YH) for x in range(XDIM)]
    left = lax.ppermute(left, ("yh", "op"), swap)
    right = lax.all_gather(right, NEAR, tiled=True)

    at = jnp.stack([plane // 2, plane % 2, position]).astype(jnp.int32)
    quarter = pl.pallas_call(
        send_kernel,
        grid_spec=pltpu.PrefetchScalarGridSpec(
            num_scalar_prefetch=1,
            grid=(1,),
            in_specs=[smem, smem, pl.BlockSpec((1, HALF, states), lambda i, at: (at[0], at[1], 0))],
            out_specs=pl.BlockSpec((YH * FROM, XROWS, WIDE), lambda i, at: (0, 0, 0)),
        ),
        out_shape=jax.ShapeDtypeStruct((YH * FROM, XROWS, WIDE), jnp.bfloat16),
        compiler_params=params,
        name="send_trial",
    )(at, left_charge, right_charge, trial_state)

    copies = jnp.broadcast_to(left[None], (YH * ZH,) + left.shape)
    sent = jnp.concatenate([quarter, copies.reshape(YH * FROM, LROWS, WIDE)], axis=1)
    sent = lax.all_to_all(sent, FAR, 0, 0, tiled=True)
    own = sent[:, XROWS:]
    other = lax.ppermute(own, "core", [(0, 1), (1, 0)])
    quarter = sent[:, :XROWS].reshape(YH, FROM * XROWS, WIDE)
    packed = jnp.concatenate(
        [quarter, jnp.broadcast_to(right[None], (XDIM,) + right.shape)], axis=1
    )
    packed = lax.all_to_all(packed, "op", 0, 0, tiled=True)

    core = lax.axis_index("core").astype(jnp.int32).reshape(1)
    partial = pl.pallas_call(
        sigma_kernel,
        grid=(2, vectors),
        in_specs=[
            smem,
            pl.BlockSpec(packed.shape, lambda g, v: (0, 0, 0)),
            pl.BlockSpec(own.shape, lambda g, v: (0, 0, 0)),
            pl.BlockSpec(own.shape, lambda g, v: (0, 0, 0)),
        ],
        out_specs=pl.BlockSpec((4, 1, BLOCK, GROUP), lambda g, v: (0, v, 0, g)),
        out_shape=jax.ShapeDtypeStruct((4, vectors, BLOCK, 2 * GROUP), jnp.bfloat16),
        scratch_shapes=[
            pltpu.VMEM((TERMS, GROUP, GROUP), jnp.bfloat16),
            pltpu.VMEM((GROUP, TERMS * GROUP), jnp.bfloat16),
            pltpu.VMEM((GROUP, TERMS * GROUP), jnp.bfloat16),
        ],
        compiler_params=params,
        name="sigma_blocks",
    )(core, packed, own, other)

    partial = lax.all_to_all(partial, NEAR, 0, 0, tiled=True)
    return pl.pallas_call(
        merge_kernel,
        grid=(vectors,),
        in_specs=[pl.BlockSpec((4, 1, BLOCK, 2 * GROUP), lambda v: (0, v, 0, 0))],
        out_specs=pl.BlockSpec((1, BLOCK, 8 * GROUP), lambda v: (v, 0, 0)),
        out_shape=jax.ShapeDtypeStruct((vectors, BLOCK, 8 * GROUP), jnp.bfloat16),
        name="merge_sectors",
    )(partial)


def solution(mesh):
    fine = Mesh(mesh.devices.reshape(YH, YL, ZH, ZL, CORE, XDIM), SEC + ("op",))
    return jax.shard_map(
        body,
        mesh=fine,
        in_specs=(
            P(None, SEC, None),
            P("op", SEC, None),
            P("op", SEC, None),
            P("op", SEC),
            P("op", SEC),
            P(),
            P(),
        ),
        out_specs=P(None, SEC, "op"),
        check_vma=False,
    )
```

```python
import jax
import jax.numpy as jnp
from jax import lax
from jax.experimental import pallas as pl
from jax.experimental.pallas import tpu as pltpu
from jax.sharding import Mesh, PartitionSpec as P

target_charge = 6
XDIM, YH, YL, ZH, ZL, CORE = 4, 4, 2, 4, 2, 2
SEC = ("yh", "yl", "zh", "zl", "core")
FAR = ("yh", "zh", "core")
NEAR = ("yl", "zl")
NT = (((1,), (1,)), ((), ()))
BLOCK = 64
WIDE = 2 * BLOCK
HALF = BLOCK // 2
GROUP = 4 * BLOCK
TERMS = 24
HERE = TERMS // XDIM
PAIRS = HERE // 2
XROWS = 2 * HALF
RROWS = PAIRS * BLOCK
FROM = ZH * CORE
VMEM = 48 * 1024 * 1024


def swap_halves(piece):
    return jnp.concatenate([piece[:, BLOCK:], piece[:, :BLOCK]], axis=1)


def placed(piece, second, to_second):
    lane = lax.broadcasted_iota(jnp.int32, piece.shape, 1)
    moved = piece if second == to_second else swap_halves(piece)
    keep = (lane >= BLOCK) if to_second else (lane < BLOCK)
    return jnp.where(keep, moved, jnp.zeros_like(moved))


def pack_kernel(lc_ref, rc_ref, left_ref, right_ref, lout_ref, rout_ref):
    for p in range(PAIRS):
        for c_ref, in_ref, out_ref in ((lc_ref, left_ref, lout_ref), (rc_ref, right_ref, rout_ref)):
            both = []
            for t in (2 * p, 2 * p + 1):
                scale = c_ref[0, t].astype(jnp.float32)
                both.append((in_ref[t].astype(jnp.float32) * scale).astype(jnp.bfloat16))
            out_ref[p * BLOCK:(p + 1) * BLOCK, :] = jnp.concatenate(both, axis=1)


def send_kernel(at_ref, x_ref, out_ref):
    for yh in range(YH):
        for yl in range(YL):
            for zh in range(ZH):
                at = ((yh * YL + yl) * ZH + zh) * ZL
                first = x_ref[0, :, at * WIDE:(at + 1) * WIDE]
                second = x_ref[0, :, (at + 1) * WIDE:(at + 2) * WIDE]
                for c in range(CORE):
                    lanes = slice(c * BLOCK, (c + 1) * BLOCK)
                    to = (yh * ZH + zh) * CORE + c
                    out_ref[to, yl * HALF:(yl + 1) * HALF, :] = jnp.concatenate(
                        [first[:, lanes], second[:, lanes]], axis=1
                    )


def spread_kernel(left_ref, after_ref, out_ref):
    for to in range(YH * ZH):
        out_ref[to] = left_ref[...]


def sigma_kernel(at_ref, lcharge_ref, rcharge_ref, xr_ref, own_ref, other_ref, out_ref, right_ref, left_ref, half_ref):
    g, v = pl.program_id(0), pl.program_id(1)
    x_at, yh_at, yl_at, zh_at, zl_at, core = [at_ref[n] for n in range(6)]

    @pl.when((g == 0) & (v == 0))
    def _():
        right_ref[...] = jnp.zeros_like(right_ref)
        left_ref[...] = jnp.zeros_like(left_ref)
        for x in range(XDIM):
            for p in range(PAIRS):
                for b in range(4):
                    at = FROM * XROWS + (b // 2) * 2 * RROWS + (b % 2) * RROWS + p * BLOCK
                    piece = xr_ref[x, at:at + BLOCK, :]
                    for s in range(2):
                        t = x * HERE + 2 * p + s
                        right_ref[t, b * BLOCK:(b + 1) * BLOCK,
                                  (b // 2) * WIDE:(b // 2 + 1) * WIDE] = placed(piece, s, b % 2)

    @pl.when(v == 0)
    def _():
        for x in range(XDIM):
            for p in range(PAIRS):
                for z in range(2):
                    rows = slice(p * BLOCK, (p + 1) * BLOCK)
                    mine = own_ref[x * ZH + g * 2 + z, rows, :]
                    theirs = other_ref[x * ZH + g * 2 + z, rows, :]
                    for c in range(CORE):
                        piece = jnp.where(core == c, mine, theirs)
                        a = z * CORE + c
                        for s in range(2):
                            t = x * HERE + 2 * p + s
                            at = t * GROUP + z * WIDE
                            left_ref[a * BLOCK:(a + 1) * BLOCK, at:at + WIDE] = placed(piece, s, c)

    rows = []
    for a in range(4):
        for h in range(2):
            start = pl.multiple_of((g * 4 + a) * XROWS, XROWS)
            piece = xr_ref[v * 2 + h, pl.ds(start, XROWS), :]
            rows.append(jnp.concatenate([piece[:HALF], piece[HALF:]], axis=1))
    state = jnp.concatenate(rows, axis=0)
    for t in range(TERMS):
        out = lax.dot_general(right_ref[t], state, NT, preferred_element_type=jnp.float32)
        half_ref[:, t * GROUP:(t + 1) * GROUP] = out.astype(half_ref.dtype)
    out = lax.dot_general(half_ref[...], left_ref[...], NT, preferred_element_type=jnp.float32)

    lane = lax.broadcasted_iota(jnp.int32, (1, GROUP), 1) // BLOCK
    charge = jnp.zeros((1, GROUP), jnp.int32)
    for a in range(4):
        sector = (((x_at * YL + yl_at) * ZH + g * 2 + a // 2) * ZL + zl_at) * CORE + a % 2
        charge = jnp.where(lane == a, lcharge_ref[sector], charge)
    for b in range(4):
        sector = (((yh_at * YL + b // 2) * ZH + zh_at) * ZL + b % 2) * CORE + core
        allowed = jnp.abs(charge + rcharge_ref[sector] - target_charge) <= 1
        block = out[b * BLOCK:(b + 1) * BLOCK]
        out_ref[b, 0] = jnp.where(allowed, block, jnp.zeros_like(block)).astype(out_ref.dtype)


def merge_kernel(in_ref, out_ref):
    for yl in range(YL):
        for zh in range(ZH):
            for zl in range(ZL):
                at = ((yl * ZH + zh) * ZL + zl) * WIDE
                out_ref[0, :, at:at + WIDE] = in_ref[yl * ZL + zl, 0, :, zh * WIDE:(zh + 1) * WIDE]


def body(
    trial_state,
    left_operators,
    right_operators,
    left_coupling,
    right_coupling,
    left_charge,
    right_charge,
):
    vectors, _, states = trial_state.shape
    at = jnp.stack([lax.axis_index(n) for n in ("op",) + SEC]).astype(jnp.int32)
    smem = pl.BlockSpec(memory_space=pltpu.SMEM)
    vmem = pl.BlockSpec(memory_space=pltpu.VMEM)
    params = pltpu.CompilerParams(vmem_limit_bytes=VMEM)

    operator = jax.ShapeDtypeStruct((RROWS, WIDE), jnp.bfloat16)
    left, right = pl.pallas_call(
        pack_kernel,
        in_specs=[smem, smem, vmem, vmem],
        out_specs=[vmem, vmem],
        out_shape=[operator, operator],
        name="pack_operators",
    )(left_coupling.reshape(1, HERE), right_coupling.reshape(1, HERE), left_operators, right_operators)
    swap = [(q * XDIM + x, x * XDIM + q) for q in range(YH) for x in range(XDIM)]
    left = lax.ppermute(left, ("yh", "op"), swap)

    quarter = pl.pallas_call(
        send_kernel,
        grid_spec=pltpu.PrefetchScalarGridSpec(
            num_scalar_prefetch=1,
            grid=(1,),
            in_specs=[
                pl.BlockSpec((1, HALF, states), lambda i, at: (at[0] // 2, lax.rem(at[0], 2), 0))
            ],
            out_specs=pl.BlockSpec((YH * FROM, XROWS, WIDE), lambda i, at: (0, 0, 0)),
        ),
        out_shape=jax.ShapeDtypeStruct((YH * FROM, XROWS, WIDE), jnp.bfloat16),
        compiler_params=params,
        name="send_trial",
    )(at, trial_state)
    quarter = lax.all_to_all(quarter, FAR, 0, 0, tiled=True)

    for axis in ("zl", "yl"):
        other = lax.ppermute(right, axis, [(0, 1), (1, 0)])
        first = lax.axis_index(axis) == 0
        right = jnp.concatenate(
            [jnp.where(first, right, other), jnp.where(first, other, right)], axis=0
        )

    left = pl.pallas_call(
        spread_kernel,
        in_specs=[vmem, pl.BlockSpec(memory_space=pl.ANY)],
        out_specs=vmem,
        out_shape=jax.ShapeDtypeStruct((YH * ZH, RROWS, WIDE), jnp.bfloat16),
        name="spread_left",
    )(left, quarter)
    own = lax.all_to_all(left, ("yh", "zh"), 0, 0, tiled=True)
    other = lax.ppermute(own, "core", [(0, 1), (1, 0)])

    quarter = quarter.reshape(YH, FROM * XROWS, WIDE)
    packed = jnp.concatenate(
        [quarter, jnp.broadcast_to(right[None], (XDIM,) + right.shape)], axis=1
    )
    packed = lax.all_to_all(packed, "op", 0, 0, tiled=True)

    partial = pl.pallas_call(
        sigma_kernel,
        grid=(2, vectors),
        in_specs=[
            smem,
            smem,
            smem,
            pl.BlockSpec(packed.shape, lambda g, v: (0, 0, 0)),
            pl.BlockSpec(own.shape, lambda g, v: (0, 0, 0)),
            pl.BlockSpec(own.shape, lambda g, v: (0, 0, 0)),
        ],
        out_specs=pl.BlockSpec((4, 1, BLOCK, GROUP), lambda g, v: (0, v, 0, g)),
        out_shape=jax.ShapeDtypeStruct((4, vectors, BLOCK, 2 * GROUP), jnp.bfloat16),
        scratch_shapes=[
            pltpu.VMEM((TERMS, GROUP, GROUP), jnp.bfloat16),
            pltpu.VMEM((GROUP, TERMS * GROUP), jnp.bfloat16),
            pltpu.VMEM((GROUP, TERMS * GROUP), jnp.bfloat16),
        ],
        compiler_params=params,
        name="sigma_blocks",
    )(at, left_charge, right_charge, packed, own, other)

    partial = lax.all_to_all(partial, NEAR, 0, 0, tiled=True)
    return pl.pallas_call(
        merge_kernel,
        grid=(vectors,),
        in_specs=[pl.BlockSpec((4, 1, BLOCK, 2 * GROUP), lambda v: (0, v, 0, 0))],
        out_specs=pl.BlockSpec((1, BLOCK, 8 * GROUP), lambda v: (v, 0, 0)),
        out_shape=jax.ShapeDtypeStruct((vectors, BLOCK, 8 * GROUP), jnp.bfloat16),
        name="merge_sectors",
    )(partial)


def solution(mesh):
    fine = Mesh(mesh.devices.reshape(YH, YL, ZH, ZL, CORE, XDIM), SEC + ("op",))
    return jax.shard_map(
        body,
        mesh=fine,
        in_specs=(
            P(None, SEC, None),
            P("op", SEC, None),
            P("op", SEC, None),
            P("op", SEC),
            P("op", SEC),
            P(),
            P(),
        ),
        out_specs=P(None, SEC, "op"),
        check_vma=False,
    )
```

```python
import jax
import jax.numpy as jnp
from jax import lax
from jax.experimental import pallas as pl
from jax.experimental.pallas import tpu as pltpu
from jax.sharding import Mesh, PartitionSpec as P

target_charge = 6
XDIM, YH, YL, ZH, ZL, CORE = 4, 4, 2, 4, 2, 2
SEC = ("yh", "yl", "zh", "zl", "core")
FAR = ("yh", "zh")
NEAR = ("yl", "zl")
NT = (((1,), (1,)), ((), ()))
BLOCK = 64
WIDE = 2 * BLOCK
HALF = BLOCK // 2
GROUP = 4 * BLOCK
TERMS = 24
HERE = TERMS // XDIM
PAIRS = HERE // 2
XROWS = 2 * HALF
RROWS = PAIRS * BLOCK
FROM = ZH * CORE
VMEM = 24 * 1024 * 1024
SMALL = 8 * 1024 * 1024


def swap_halves(piece):
    return jnp.concatenate([piece[:, BLOCK:], piece[:, :BLOCK]], axis=1)


def placed(piece, second, to_second):
    lane = lax.broadcasted_iota(jnp.int32, piece.shape, 1)
    moved = piece if second == to_second else swap_halves(piece)
    keep = (lane >= BLOCK) if to_second else (lane < BLOCK)
    return jnp.where(keep, moved, jnp.zeros_like(moved))


def prepare_kernel(at_ref, lc_ref, rc_ref, left_ref, right_ref, x_ref, sent_ref, rout_ref):
    wide = CORE * XROWS
    for p in range(PAIRS):
        pairs = []
        for c_ref, in_ref in ((lc_ref, left_ref), (rc_ref, right_ref)):
            both = []
            for t in (2 * p, 2 * p + 1):
                scale = c_ref[0, t].astype(jnp.float32)
                both.append((in_ref[t].astype(jnp.float32) * scale).astype(jnp.bfloat16))
            pairs.append(jnp.concatenate(both, axis=1))
        rout_ref[p * BLOCK:(p + 1) * BLOCK, :] = pairs[1]
        for to in range(YH * ZH):
            sent_ref[to, wide + p * BLOCK:wide + (p + 1) * BLOCK, :] = pairs[0]
    for yh in range(YH):
        for yl in range(YL):
            for zh in range(ZH):
                at = ((yh * YL + yl) * ZH + zh) * ZL
                first = x_ref[0, :, at * WIDE:(at + 1) * WIDE]
                second = x_ref[0, :, (at + 1) * WIDE:(at + 2) * WIDE]
                for c in range(CORE):
                    lanes = slice(c * BLOCK, (c + 1) * BLOCK)
                    rows = slice(c * XROWS + yl * HALF, c * XROWS + (yl + 1) * HALF)
                    sent_ref[yh * ZH + zh, rows, :] = jnp.concatenate(
                        [first[:, lanes], second[:, lanes]], axis=1
                    )


def plane_kernel(got_ref, r0_ref, r1_ref, r2_ref, r3_ref, out_ref, right_ref):
    wide = CORE * XROWS
    for at in range(YH * ZH):
        q, z = at // ZH, at % ZH
        out_ref[q, z * wide:(z + 1) * wide, :] = got_ref[at, :wide, :]
        rows = slice(ZH * wide + z * RROWS, ZH * wide + (z + 1) * RROWS)
        out_ref[q, rows, :] = got_ref[at, wide:, :]
    for d, ref in enumerate((r0_ref, r1_ref, r2_ref, r3_ref)):
        right_ref[d * RROWS:(d + 1) * RROWS, :] = ref[...]


def core_kernel(at_ref, got_ref, r0_ref, r1_ref, r2_ref, r3_ref, own_ref, give_ref, near_ref):
    core = at_ref[5]
    for e, ref in enumerate((r0_ref, r1_ref, r2_ref, r3_ref)):
        near_ref[jnp.bitwise_xor(at_ref[2] * ZL + at_ref[4], e)] = ref[...]
    for x in range(XDIM):
        for z in range(ZH):
            rows = slice(z * XROWS, (z + 1) * XROWS)
            for to_ref, c in ((own_ref, core), (give_ref, 1 - core)):
                at = pl.multiple_of((z * CORE + c) * XROWS, XROWS)
                to_ref[x, rows, :] = got_ref[x, pl.ds(at, XROWS), :]
        left = got_ref[x, FROM * XROWS:, :]
        own_ref[x, ZH * XROWS:, :] = left
        give_ref[x, ZH * XROWS:, :] = left


def sigma_kernel(c, at_ref, lcharge_ref, rcharge_ref, got_ref, near_ref, *refs):
    out_ref, right_ref, left_ref, half_ref = refs[-4:]
    v = pl.program_id(0)
    x_at, yh_at, yl_at, zh_at, zl_at, core = [at_ref[n] for n in range(6)]

    @pl.when(v == 0)
    def _():
        right_ref[...] = jnp.zeros_like(right_ref)
        left_ref[...] = jnp.zeros_like(left_ref)
        for b in range(4):
            for d in range(XDIM):
                first = jnp.bitwise_xor(x_at, d) * HERE
                for p in range(PAIRS):
                    at = d * RROWS + p * BLOCK
                    piece = near_ref[b, at:at + BLOCK, :]
                    for s in range(2):
                        right_ref[first + 2 * p + s, b * BLOCK:(b + 1) * BLOCK,
                                  (b // 2) * WIDE:(b // 2 + 1) * WIDE] = placed(piece, s, b % 2)
        for x in range(XDIM):
            for z in range(ZH):
                for p in range(PAIRS):
                    at = ZH * XROWS + z * RROWS + p * BLOCK
                    piece = got_ref[x, at:at + BLOCK, :]
                    for s in range(2):
                        at = (x * HERE + 2 * p + s) * GROUP + (z // 2) * WIDE
                        left_ref[z * BLOCK:(z + 1) * BLOCK, at:at + WIDE] = placed(piece, s, z % 2)

    rows = []
    for z in range(ZH):
        for h in range(2):
            piece = got_ref[v * 2 + h, z * XROWS:(z + 1) * XROWS, :]
            rows.append(jnp.concatenate([piece[:HALF], piece[HALF:]], axis=1))
    state = jnp.concatenate(rows, axis=0)
    for t in range(TERMS):
        out = lax.dot_general(right_ref[t], state, NT, preferred_element_type=jnp.float32)
        half_ref[:, t * GROUP:(t + 1) * GROUP] = out.astype(half_ref.dtype)
    out = lax.dot_general(half_ref[...], left_ref[...], NT, preferred_element_type=jnp.float32)

    lane = lax.broadcasted_iota(jnp.int32, (1, GROUP), 1) // BLOCK
    charge = jnp.zeros((1, GROUP), jnp.int32)
    for z in range(ZH):
        sector = (((x_at * YL + yl_at) * ZH + z) * ZL + zl_at) * CORE + jnp.bitwise_xor(core, c)
        charge = jnp.where(lane == z, lcharge_ref[sector], charge)
    for b in range(4):
        sector = (((yh_at * YL + b // 2) * ZH + zh_at) * ZL + b % 2) * CORE + core
        allowed = jnp.abs(charge + rcharge_ref[sector] - target_charge) <= 1
        block = out[b * BLOCK:(b + 1) * BLOCK]
        out_ref[b, 0, 0] = jnp.where(allowed, block, jnp.zeros_like(block)).astype(out_ref.dtype)


def merge_kernel(at_ref, in_ref, out_ref):
    core = at_ref[5]
    for yl in range(YL):
        for zl in range(ZL):
            for m in range(ZH // 2):
                low = in_ref[yl * ZL + zl, core, 0, :, m * WIDE:(m + 1) * WIDE]
                high = in_ref[yl * ZL + zl, 1 - core, 0, :, m * WIDE:(m + 1) * WIDE]
                for h in range(2):
                    lanes = slice(h * BLOCK, (h + 1) * BLOCK)
                    at = ((yl * ZH + 2 * m + h) * ZL + zl) * WIDE
                    out_ref[0, :, at:at + WIDE] = jnp.concatenate(
                        [low[:, lanes], high[:, lanes]], axis=1
                    )


def body(
    trial_state,
    left_operators,
    right_operators,
    left_coupling,
    right_coupling,
    left_charge,
    right_charge,
):
    vectors, _, states = trial_state.shape
    at = jnp.stack([lax.axis_index(n) for n in ("op",) + SEC]).astype(jnp.int32)
    smem = pl.BlockSpec(memory_space=pltpu.SMEM)
    vmem = pl.BlockSpec(memory_space=pltpu.VMEM)
    params = pltpu.CompilerParams(vmem_limit_bytes=VMEM)
    small = pltpu.CompilerParams(vmem_limit_bytes=SMALL)

    wide = CORE * XROWS
    message = jax.ShapeDtypeStruct((YH * ZH, wide + RROWS, WIDE), jnp.bfloat16)
    operator = jax.ShapeDtypeStruct((RROWS, WIDE), jnp.bfloat16)

    def whole(shape):
        return pl.BlockSpec(shape, lambda i, at: (0,) * len(shape))

    sent, right = pl.pallas_call(
        prepare_kernel,
        grid_spec=pltpu.PrefetchScalarGridSpec(
            num_scalar_prefetch=1,
            grid=(1,),
            in_specs=[
                smem,
                smem,
                whole(left_operators.shape),
                whole(right_operators.shape),
                pl.BlockSpec((1, HALF, states), lambda i, at: (at[0] // 2, lax.rem(at[0], 2), 0)),
            ],
            out_specs=[whole(message.shape), whole(operator.shape)],
        ),
        out_shape=[message, operator],
        name="prepare_parts",
    )(
        at,
        left_coupling.reshape(1, HERE),
        right_coupling.reshape(1, HERE),
        left_operators,
        right_operators,
        trial_state,
    )
    got = lax.all_to_all(sent, FAR, 0, 0, tiled=True)

    rights = [right] + [
        lax.ppermute(right, "op", [(n, n ^ d) for n in range(XDIM)]) for d in (1, 2, 3)
    ]

    plane = jax.ShapeDtypeStruct((XDIM, ZH * message.shape[1], WIDE), jnp.bfloat16)
    got, right = pl.pallas_call(
        plane_kernel,
        in_specs=[vmem] * 5,
        out_specs=[vmem] * 2,
        out_shape=[plane, jax.ShapeDtypeStruct((XDIM * RROWS, WIDE), jnp.bfloat16)],
        compiler_params=small,
        name="sort_planes",
    )(got, *rights)
    got = lax.all_to_all(got, "op", 0, 0, tiled=True)

    rights = [right] + [
        lax.ppermute(right, NEAR, [(n, n ^ d) for n in range(YL * ZL)]) for d in (1, 2, 3)
    ]

    mine = jax.ShapeDtypeStruct((XDIM, ZH * (XROWS + RROWS), WIDE), jnp.bfloat16)
    near = jax.ShapeDtypeStruct((YL * ZL,) + right.shape, jnp.bfloat16)
    own, give, right = pl.pallas_call(
        core_kernel,
        in_specs=[smem] + [vmem] * 5,
        out_specs=[vmem] * 3,
        out_shape=[mine, mine, near],
        compiler_params=small,
        name="sort_cores",
    )(at, got, *rights)
    other = lax.ppermute(give, "core", [(0, 1), (1, 0)])

    partial = None
    for c, got in enumerate((own, other)):
        before = [] if partial is None else [partial]
        partial = pl.pallas_call(
            lambda *refs, c=c: sigma_kernel(c, *refs),
            grid=(vectors,),
            in_specs=[smem] * 3
            + [pl.BlockSpec(mine.shape, lambda v: (0, 0, 0))]
            + [pl.BlockSpec(near.shape, lambda v: (0, 0, 0))]
            + [pl.BlockSpec(memory_space=pl.ANY) for _ in before],
            out_specs=pl.BlockSpec((4, 1, 1, BLOCK, GROUP), lambda v, c=c: (0, c, v, 0, 0)),
            out_shape=jax.ShapeDtypeStruct((4, CORE, vectors, BLOCK, GROUP), jnp.bfloat16),
            scratch_shapes=[
                pltpu.VMEM((TERMS, GROUP, GROUP), jnp.bfloat16),
                pltpu.VMEM((GROUP, TERMS * GROUP), jnp.bfloat16),
                pltpu.VMEM((GROUP, TERMS * GROUP), jnp.bfloat16),
            ],
            input_output_aliases={5: 0} if before else {},
            compiler_params=params,
            name="sigma_blocks",
        )(at, left_charge, right_charge, got, right, *before)

    partial = lax.all_to_all(partial, NEAR, 0, 0, tiled=True)
    return pl.pallas_call(
        merge_kernel,
        grid=(vectors,),
        in_specs=[
            smem,
            pl.BlockSpec((4, CORE, 1, BLOCK, GROUP), lambda v: (0, 0, v, 0, 0)),
        ],
        out_specs=pl.BlockSpec((1, BLOCK, 8 * GROUP), lambda v: (v, 0, 0)),
        out_shape=jax.ShapeDtypeStruct((vectors, BLOCK, 8 * GROUP), jnp.bfloat16),
        compiler_params=small,
        name="merge_sectors",
    )(at, partial)


def solution(mesh):
    fine = Mesh(mesh.devices.reshape(YH, YL, ZH, ZL, CORE, XDIM), SEC + ("op",))
    return jax.shard_map(
        body,
        mesh=fine,
        in_specs=(
            P(None, SEC, None),
            P("op", SEC, None),
            P("op", SEC, None),
            P("op", SEC),
            P("op", SEC),
            P(),
            P(),
        ),
        out_specs=P(None, SEC, "op"),
        check_vma=False,
    )
```

```python
import jax
import jax.numpy as jnp
from jax import lax
from jax.experimental import pallas as pl
from jax.experimental.pallas import tpu as pltpu
from jax.sharding import Mesh, PartitionSpec as P

target_charge = 6
XDIM, YH, YL, ZH, ZL, CORE = 4, 4, 2, 4, 2, 2
SEC = ("yh", "yl", "zh", "zl", "core")
FAR = ("yh", "zh")
NEAR = ("yl", "zl")
NT = (((1,), (1,)), ((), ()))
BLOCK = 64
WIDE = 2 * BLOCK
HALF = BLOCK // 2
GROUP = 4 * BLOCK
TERMS = 24
HERE = TERMS // XDIM
PAIRS = HERE // 2
XROWS = 2 * HALF
RROWS = PAIRS * BLOCK
FROM = ZH * CORE
VMEM = 24 * 1024 * 1024
SMALL = 8 * 1024 * 1024


def swap_halves(piece):
    return jnp.concatenate([piece[:, BLOCK:], piece[:, :BLOCK]], axis=1)


def placed(piece, second, to_second):
    lane = lax.broadcasted_iota(jnp.int32, piece.shape, 1)
    moved = piece if second == to_second else swap_halves(piece)
    keep = (lane >= BLOCK) if to_second else (lane < BLOCK)
    return jnp.where(keep, moved, jnp.zeros_like(moved))


def place():
    return [lax.axis_index(n).astype(jnp.int32) for n in ("op",) + SEC]


def prepare_kernel(
    lc_ref, rc_ref, left_in, right_in, x_ref, out_ref, rout_ref,
    sent_ref, left_ref, right_ref, rows_ref, sems,
):
    operators = [
        pltpu.make_async_copy(source, ref, sems.at[YH + n])
        for n, (source, ref) in enumerate(((left_in, left_ref), (right_in, right_ref)))
    ]
    for copy in operators:
        copy.start()
    plane = lax.axis_index("op").astype(jnp.int32)
    lanes_of = rows_ref.shape[2]
    copies = []
    for yh in range(YH):
        source = x_ref.at[
            plane // 2,
            pl.ds(pl.multiple_of(lax.rem(plane, 2) * HALF, HALF), HALF),
            pl.ds(yh * lanes_of, lanes_of),
        ]
        copies.append(pltpu.make_async_copy(source, rows_ref.at[yh], sems.at[yh]))
        copies[-1].start()
    for copy in operators:
        copy.wait()
    wide = CORE * XROWS
    for p in range(PAIRS):
        pairs = []
        for c_ref, in_ref in ((lc_ref, left_ref), (rc_ref, right_ref)):
            both = []
            for t in (2 * p, 2 * p + 1):
                scale = c_ref[0, t].astype(jnp.float32)
                both.append((in_ref[t].astype(jnp.float32) * scale).astype(jnp.bfloat16))
            pairs.append(jnp.concatenate(both, axis=1))
        rout_ref[p * BLOCK:(p + 1) * BLOCK, :] = pairs[1]
        for to in range(YH * ZH):
            sent_ref[to, wide + p * BLOCK:wide + (p + 1) * BLOCK, :] = pairs[0]
    for yh in range(YH):
        copies[yh].wait()
        for yl in range(YL):
            for zh in range(ZH):
                at = (yl * ZH + zh) * ZL
                first = rows_ref[yh, :, at * WIDE:(at + 1) * WIDE]
                second = rows_ref[yh, :, (at + 1) * WIDE:(at + 2) * WIDE]
                for c in range(CORE):
                    lanes = slice(c * BLOCK, (c + 1) * BLOCK)
                    rows = slice(c * XROWS + yl * HALF, c * XROWS + (yl + 1) * HALF)
                    sent_ref[yh * ZH + zh, rows, :] = jnp.concatenate(
                        [first[:, lanes], second[:, lanes]], axis=1
                    )
        done = pl.ds(yh * ZH, ZH)
        copies.append(
            pltpu.make_async_copy(sent_ref.at[done], out_ref.at[done], sems.at[YH + 2 + yh])
        )
        copies[-1].start()
    for copy in copies[YH:]:
        copy.wait()


def stack_kernel(got_ref, r0_ref, r1_ref, r2_ref, r3_ref, same_ref, right_ref):
    for d, ref in enumerate((r0_ref, r1_ref, r2_ref, r3_ref)):
        right_ref[d * RROWS:(d + 1) * RROWS, :] = ref[...]


def core_kernel(got_ref, r0_ref, r1_ref, r2_ref, r3_ref, own_ref, give_ref, near_ref):
    _, _, yl_at, _, zl_at, core = place()
    for e, ref in enumerate((r0_ref, r1_ref, r2_ref, r3_ref)):
        near_ref[jnp.bitwise_xor(yl_at * ZL + zl_at, e)] = ref[...]
    step = CORE * XROWS + RROWS
    for x in range(XDIM):
        for z in range(ZH):
            rows = slice(z * XROWS, (z + 1) * XROWS)
            for to_ref, c in ((own_ref, core), (give_ref, 1 - core)):
                at = pl.multiple_of(z * step + c * XROWS, XROWS)
                to_ref[x, rows, :] = got_ref[x, pl.ds(at, XROWS), :]
            left = got_ref[x, z * step + CORE * XROWS:(z + 1) * step, :]
            rows = slice(ZH * XROWS + z * RROWS, ZH * XROWS + (z + 1) * RROWS)
            own_ref[x, rows, :] = left
            give_ref[x, rows, :] = left


def build_right(x_at, near_ref, right_ref):
    zeros = jnp.zeros((BLOCK, WIDE), jnp.bfloat16)
    for b in range(4):
        rows = slice(b * BLOCK, (b + 1) * BLOCK)
        used = slice((b // 2) * WIDE, (b // 2 + 1) * WIDE)
        unused = slice((1 - b // 2) * WIDE, (2 - b // 2) * WIDE)
        for d in range(XDIM):
            first = jnp.bitwise_xor(x_at, d) * HERE
            for p in range(PAIRS):
                at = d * RROWS + p * BLOCK
                piece = near_ref[b, at:at + BLOCK, :]
                for s in range(2):
                    right_ref[first + 2 * p + s, rows, used] = placed(piece, s, b % 2)
                    right_ref[first + 2 * p + s, rows, unused] = zeros


def build_left(got_ref, left_ref):
    zeros = jnp.zeros((BLOCK, WIDE), jnp.bfloat16)
    for x in range(XDIM):
        for z in range(ZH):
            rows = slice(z * BLOCK, (z + 1) * BLOCK)
            for p in range(PAIRS):
                at = ZH * XROWS + z * RROWS + p * BLOCK
                piece = got_ref[x, at:at + BLOCK, :]
                for s in range(2):
                    at = (x * HERE + 2 * p + s) * GROUP
                    used, unused = at + (z // 2) * WIDE, at + (1 - z // 2) * WIDE
                    left_ref[rows, used:used + WIDE] = placed(piece, s, z % 2)
                    left_ref[rows, unused:unused + WIDE] = zeros


def sigma_kernel(c, lcharge_ref, rcharge_ref, got_ref, near_ref, *refs):
    if c == 0:
        out_ref, right_ref, left_ref, half_ref = refs
    else:
        right_ref, _, out_ref, left_ref, half_ref = refs
    x_at, yh_at, yl_at, zh_at, zl_at, core = place()
    if c == 0:
        build_right(x_at, near_ref, right_ref)
    vectors = half_ref.shape[0] // GROUP
    for v in range(vectors):
        rows = []
        for z in range(ZH):
            for h in range(2):
                piece = got_ref[v * 2 + h, z * XROWS:(z + 1) * XROWS, :]
                rows.append(jnp.concatenate([piece[:HALF], piece[HALF:]], axis=1))
        state = jnp.concatenate(rows, axis=0)
        for t in range(TERMS):
            out = lax.dot_general(right_ref[t], state, NT, preferred_element_type=jnp.float32)
            half_ref[v * GROUP:(v + 1) * GROUP, t * GROUP:(t + 1) * GROUP] = out.astype(
                half_ref.dtype
            )
    build_left(got_ref, left_ref)
    out = lax.dot_general(half_ref[...], left_ref[...], NT, preferred_element_type=jnp.float32)

    lane = lax.broadcasted_iota(jnp.int32, (1, GROUP), 1) // BLOCK
    charge = jnp.zeros((1, GROUP), jnp.int32)
    for z in range(ZH):
        sector = (((x_at * YL + yl_at) * ZH + z) * ZL + zl_at) * CORE + jnp.bitwise_xor(core, c)
        charge = jnp.where(lane == z, lcharge_ref[sector], charge)
    for b in range(4):
        sector = (((yh_at * YL + b // 2) * ZH + zh_at) * ZL + b % 2) * CORE + core
        allowed = jnp.abs(charge + rcharge_ref[sector] - target_charge) <= 1
        for v in range(vectors):
            at = v * GROUP + b * BLOCK
            block = out[at:at + BLOCK]
            out_ref[b, 0, v] = jnp.where(allowed, block, jnp.zeros_like(block)).astype(
                out_ref.dtype
            )


def merge_kernel(in_ref, out_ref):
    core = lax.axis_index("core").astype(jnp.int32)
    for yl in range(YL):
        for zl in range(ZL):
            for m in range(ZH // 2):
                low = in_ref[yl * ZL + zl, core, 0, :, m * WIDE:(m + 1) * WIDE]
                high = in_ref[yl * ZL + zl, 1 - core, 0, :, m * WIDE:(m + 1) * WIDE]
                for h in range(2):
                    lanes = slice(h * BLOCK, (h + 1) * BLOCK)
                    at = ((yl * ZH + 2 * m + h) * ZL + zl) * WIDE
                    out_ref[0, :, at:at + WIDE] = jnp.concatenate(
                        [low[:, lanes], high[:, lanes]], axis=1
                    )


def body(
    trial_state,
    left_operators,
    right_operators,
    left_coupling,
    right_coupling,
    left_charge,
    right_charge,
):
    vectors, _, states = trial_state.shape
    smem = pl.BlockSpec(memory_space=pltpu.SMEM)
    vmem = pl.BlockSpec(memory_space=pltpu.VMEM)
    anywhere = pl.BlockSpec(memory_space=pl.ANY)
    params = pltpu.CompilerParams(vmem_limit_bytes=VMEM)
    small = pltpu.CompilerParams(vmem_limit_bytes=SMALL)

    wide = CORE * XROWS
    message = jax.ShapeDtypeStruct((YH * ZH, wide + RROWS, WIDE), jnp.bfloat16)
    operator = jax.ShapeDtypeStruct((RROWS, WIDE), jnp.bfloat16)

    sent, right = pl.pallas_call(
        prepare_kernel,
        in_specs=[smem, smem] + [pl.BlockSpec(memory_space=pltpu.HBM)] * 3,
        out_specs=[anywhere, vmem],
        out_shape=[message, operator],
        scratch_shapes=[
            pltpu.VMEM(message.shape, jnp.bfloat16),
            pltpu.VMEM(left_operators.shape, jnp.bfloat16),
            pltpu.VMEM(right_operators.shape, jnp.bfloat16),
            pltpu.VMEM((YH, HALF, states // YH), jnp.bfloat16),
            pltpu.SemaphoreType.DMA((2 * YH + 2,)),
        ],
        name="prepare_parts",
    )(
        left_coupling.reshape(1, HERE),
        right_coupling.reshape(1, HERE),
        left_operators,
        right_operators,
        trial_state,
    )
    got = lax.all_to_all(sent, FAR, 0, 0, tiled=True)

    rights = [right] + [
        lax.ppermute(right, "op", [(n, n ^ d) for n in range(XDIM)]) for d in (1, 2, 3)
    ]

    got, right = pl.pallas_call(
        stack_kernel,
        in_specs=[anywhere] + [vmem] * 4,
        out_specs=[anywhere, vmem],
        out_shape=[message, jax.ShapeDtypeStruct((XDIM * RROWS, WIDE), jnp.bfloat16)],
        input_output_aliases={0: 0},
        compiler_params=small,
        name="stack_right",
    )(got, *rights)

    got = got.reshape(XDIM, ZH * message.shape[1], WIDE)
    got = lax.all_to_all(got, "op", 0, 0, tiled=True)

    rights = [right] + [
        lax.ppermute(right, NEAR, [(n, n ^ d) for n in range(YL * ZL)]) for d in (1, 2, 3)
    ]

    mine = jax.ShapeDtypeStruct((XDIM, ZH * (XROWS + RROWS), WIDE), jnp.bfloat16)
    near = jax.ShapeDtypeStruct((YL * ZL,) + right.shape, jnp.bfloat16)
    own, give, right = pl.pallas_call(
        core_kernel,
        in_specs=[vmem] * 5,
        out_specs=[vmem] * 3,
        out_shape=[mine, mine, near],
        compiler_params=small,
        name="sort_cores",
    )(got, *rights)
    other = lax.ppermute(give, "core", [(0, 1), (1, 0)])

    shared = [
        jax.ShapeDtypeStruct((TERMS, GROUP, GROUP), jnp.bfloat16),
        jax.ShapeDtypeStruct((4, CORE, vectors, BLOCK, GROUP), jnp.bfloat16),
    ]
    blocks = [
        pl.BlockSpec((4, 1, vectors, BLOCK, GROUP), lambda i, c=c: (0, c, 0, 0, 0))
        for c in range(CORE)
    ]
    keep = pl.BlockSpec(shared[0].shape, lambda v: (0, 0, 0))
    scratch = [
        pltpu.VMEM((GROUP, TERMS * GROUP), jnp.bfloat16),
        pltpu.VMEM((vectors * GROUP, TERMS * GROUP), jnp.bfloat16),
    ]
    inputs = [smem, smem] + [
        pl.BlockSpec(shape.shape, lambda v: (0, 0, 0)) for shape in (mine, near)
    ]
    partial, diagonal = pl.pallas_call(
        lambda *refs: sigma_kernel(0, *refs),
        grid=(1,),
        in_specs=inputs,
        out_specs=[blocks[0], keep],
        out_shape=shared[::-1],
        scratch_shapes=scratch,
        compiler_params=params,
        name="sigma_own",
    )(left_charge, right_charge, own, right)
    partial = pl.pallas_call(
        lambda lc, rc, got, *refs: sigma_kernel(1, lc, rc, got, None, *refs),
        grid=(1,),
        in_specs=inputs[:3] + [keep, anywhere],
        out_specs=blocks[1],
        out_shape=shared[1],
        scratch_shapes=scratch,
        input_output_aliases={4: 0},
        compiler_params=params,
        name="sigma_other",
    )(left_charge, right_charge, other, diagonal, partial)

    partial = lax.all_to_all(partial, NEAR, 0, 0, tiled=True)
    return pl.pallas_call(
        merge_kernel,
        grid=(vectors,),
        in_specs=[pl.BlockSpec((4, CORE, 1, BLOCK, GROUP), lambda v: (0, 0, v, 0, 0))],
        out_specs=pl.BlockSpec((1, BLOCK, 8 * GROUP), lambda v: (v, 0, 0)),
        out_shape=jax.ShapeDtypeStruct((vectors, BLOCK, 8 * GROUP), jnp.bfloat16),
        compiler_params=small,
        name="merge_sectors",
    )(partial)


def solution(mesh):
    fine = Mesh(mesh.devices.reshape(YH, YL, ZH, ZL, CORE, XDIM), SEC + ("op",))
    return jax.shard_map(
        body,
        mesh=fine,
        in_specs=(
            P(None, SEC, None),
            P("op", SEC, None),
            P("op", SEC, None),
            P("op", SEC),
            P("op", SEC),
            P(),
            P(),
        ),
        out_specs=P(None, SEC, "op"),
        check_vma=False,
    )
```

```python
import jax
import jax.numpy as jnp
from jax import lax
from jax.experimental import pallas as pl
from jax.experimental.pallas import tpu as pltpu
from jax.sharding import Mesh, PartitionSpec as P

target_charge = 6
XDIM, YH, YL, ZH, ZL, CORE = 4, 4, 2, 4, 2, 2
SEC = ("yh", "yl", "zh", "zl", "core")
FAR = ("yh", "zh")
NEAR = ("yl", "zl")
NT = (((1,), (1,)), ((), ()))
BLOCK = 64
WIDE = 2 * BLOCK
HALF = BLOCK // 2
GROUP = 4 * BLOCK
TERMS = 24
HERE = TERMS // XDIM
PAIRS = HERE // 2
XROWS = 2 * HALF
RROWS = PAIRS * BLOCK
FROM = ZH * CORE
VMEM = 24 * 1024 * 1024
SMALL = 8 * 1024 * 1024


def swap_halves(piece):
    return jnp.concatenate([piece[:, BLOCK:], piece[:, :BLOCK]], axis=1)


def placed(piece, second, to_second):
    lane = lax.broadcasted_iota(jnp.int32, piece.shape, 1)
    moved = piece if second == to_second else swap_halves(piece)
    keep = (lane >= BLOCK) if to_second else (lane < BLOCK)
    return jnp.where(keep, moved, jnp.zeros_like(moved))


def place():
    return [lax.axis_index(n).astype(jnp.int32) for n in ("op",) + SEC]


def prepare_kernel(
    lc_in, rc_in, left_in, right_in, x_ref, out_ref, lout_ref, rout_ref,
    sent_ref, lc_ref, rc_ref, left_ref, right_ref, rows_ref, sems,
):
    plane = lax.axis_index("op").astype(jnp.int32)
    lanes_of = rows_ref.shape[2]
    copies = []

    def copy(source, to):
        copies.append(pltpu.make_async_copy(source, to, sems.at[len(copies)]))
        copies[-1].start()

    for yh in range(YH):
        source = x_ref.at[
            plane // 2,
            pl.ds(pl.multiple_of(lax.rem(plane, 2) * HALF, HALF), HALF),
            pl.ds(yh * lanes_of, lanes_of),
        ]
        copy(source, rows_ref.at[yh])
    copy(left_in, left_ref)
    copy(right_in, right_ref)
    copy(lc_in, lc_ref)
    copy(rc_in, rc_ref)
    for yh in range(YH):
        copies[yh].wait()
        for yl in range(YL):
            for zh in range(ZH):
                at = (yl * ZH + zh) * ZL
                first = rows_ref[yh, :, at * WIDE:(at + 1) * WIDE]
                second = rows_ref[yh, :, (at + 1) * WIDE:(at + 2) * WIDE]
                for c in range(CORE):
                    lanes = slice(c * BLOCK, (c + 1) * BLOCK)
                    rows = slice(c * XROWS + yl * HALF, c * XROWS + (yl + 1) * HALF)
                    sent_ref[yh * ZH + zh, rows, :] = jnp.concatenate(
                        [first[:, lanes], second[:, lanes]], axis=1
                    )
        places = pl.ds(yh * ZH, ZH)
        copy(sent_ref.at[places], out_ref.at[places])
    for n, (c_ref, in_ref, to_ref) in enumerate(
        ((lc_ref, left_ref, lout_ref), (rc_ref, right_ref, rout_ref))
    ):
        copies[YH + n].wait()
        copies[YH + 2 + n].wait()
        scale = c_ref[...].astype(jnp.float32)
        for p in range(PAIRS):
            both = []
            for t in (2 * p, 2 * p + 1):
                scaled = in_ref[t].astype(jnp.float32) * scale[:, t:t + 1]
                both.append(scaled.astype(jnp.bfloat16))
            to_ref[p * BLOCK:(p + 1) * BLOCK, :] = jnp.concatenate(both, axis=1)
    for done in copies[YH + 4:]:
        done.wait()


def spread_kernel(
    got_ref, left_ref, r0_ref, r1_ref, r2_ref, r3_ref,
    x0_ref, x1_ref, x2_ref, x3_ref, sent_ref, right_ref,
):
    plane = lax.axis_index("op").astype(jnp.int32)
    wide = CORE * XROWS
    for d, ref in enumerate((x0_ref, x1_ref, x2_ref, x3_ref)):
        to = jnp.bitwise_xor(plane, d)
        for z in range(ZH):
            ref[z * wide:(z + 1) * wide, :] = got_ref[to * ZH + z]
    for to in range(YH * ZH):
        sent_ref[to] = left_ref[...]
    for d, ref in enumerate((r0_ref, r1_ref, r2_ref, r3_ref)):
        right_ref[d * RROWS:(d + 1) * RROWS, :] = ref[...]


def core_kernel(
    left_ref, x0_ref, x1_ref, x2_ref, x3_ref, r0_ref, r1_ref, r2_ref, r3_ref,
    own_ref, give_ref, near_ref,
):
    x_at, _, yl_at, _, zl_at, core = place()
    for e, ref in enumerate((r0_ref, r1_ref, r2_ref, r3_ref)):
        near_ref[jnp.bitwise_xor(yl_at * ZL + zl_at, e)] = ref[...]
    for d, ref in enumerate((x0_ref, x1_ref, x2_ref, x3_ref)):
        x = jnp.bitwise_xor(x_at, d)
        for z in range(ZH):
            rows = slice(z * XROWS, (z + 1) * XROWS)
            for to_ref, c in ((own_ref, core), (give_ref, 1 - core)):
                at = pl.multiple_of((z * CORE + c) * XROWS, XROWS)
                to_ref[x, rows, :] = ref[pl.ds(at, XROWS), :]
    for x in range(XDIM):
        for z in range(ZH):
            rows = slice(ZH * XROWS + z * RROWS, ZH * XROWS + (z + 1) * RROWS)
            left = left_ref[x * ZH + z]
            own_ref[x, rows, :] = left
            give_ref[x, rows, :] = left


def build_right(x_at, near_ref, right_ref):
    zeros = jnp.zeros((BLOCK, WIDE), jnp.bfloat16)
    for b in range(4):
        rows = slice(b * BLOCK, (b + 1) * BLOCK)
        used = slice((b // 2) * WIDE, (b // 2 + 1) * WIDE)
        unused = slice((1 - b // 2) * WIDE, (2 - b // 2) * WIDE)
        for d in range(XDIM):
            first = jnp.bitwise_xor(x_at, d) * HERE
            for p in range(PAIRS):
                at = d * RROWS + p * BLOCK
                piece = near_ref[b, at:at + BLOCK, :]
                for s in range(2):
                    right_ref[first + 2 * p + s, rows, used] = placed(piece, s, b % 2)
                    right_ref[first + 2 * p + s, rows, unused] = zeros


def build_left(got_ref, left_ref):
    zeros = jnp.zeros((BLOCK, WIDE), jnp.bfloat16)
    for x in range(XDIM):
        for z in range(ZH):
            rows = slice(z * BLOCK, (z + 1) * BLOCK)
            for p in range(PAIRS):
                at = ZH * XROWS + z * RROWS + p * BLOCK
                piece = got_ref[x, at:at + BLOCK, :]
                for s in range(2):
                    at = (x * HERE + 2 * p + s) * GROUP
                    used, unused = at + (z // 2) * WIDE, at + (1 - z // 2) * WIDE
                    left_ref[rows, used:used + WIDE] = placed(piece, s, z % 2)
                    left_ref[rows, unused:unused + WIDE] = zeros


def sigma_kernel(c, lcharge_ref, rcharge_ref, got_ref, near_ref, *refs):
    if c == 0:
        out_ref, right_ref, left_ref, half_ref = refs
    else:
        right_ref, _, out_ref, left_ref, half_ref = refs
    x_at, yh_at, yl_at, zh_at, zl_at, core = place()
    if c == 0:
        build_right(x_at, near_ref, right_ref)
    vectors = half_ref.shape[0] // GROUP
    for v in range(vectors):
        rows = []
        for z in range(ZH):
            for h in range(2):
                piece = got_ref[v * 2 + h, z * XROWS:(z + 1) * XROWS, :]
                rows.append(jnp.concatenate([piece[:HALF], piece[HALF:]], axis=1))
        state = jnp.concatenate(rows, axis=0)
        for t in range(TERMS):
            out = lax.dot_general(right_ref[t], state, NT, preferred_element_type=jnp.float32)
            half_ref[v * GROUP:(v + 1) * GROUP, t * GROUP:(t + 1) * GROUP] = out.astype(
                half_ref.dtype
            )
    build_left(got_ref, left_ref)
    out = lax.dot_general(half_ref[...], left_ref[...], NT, preferred_element_type=jnp.float32)

    lane = lax.broadcasted_iota(jnp.int32, (1, GROUP), 1) // BLOCK
    charge = jnp.zeros((1, GROUP), jnp.int32)
    for z in range(ZH):
        sector = (((x_at * YL + yl_at) * ZH + z) * ZL + zl_at) * CORE + jnp.bitwise_xor(core, c)
        charge = jnp.where(lane == z, lcharge_ref[sector], charge)
    for b in range(4):
        sector = (((yh_at * YL + b // 2) * ZH + zh_at) * ZL + b % 2) * CORE + core
        allowed = jnp.abs(charge + rcharge_ref[sector] - target_charge) <= 1
        for v in range(vectors):
            at = v * GROUP + b * BLOCK
            block = out[at:at + BLOCK]
            out_ref[b, 0, v] = jnp.where(allowed, block, jnp.zeros_like(block)).astype(
                out_ref.dtype
            )


def merge_kernel(in_ref, out_ref):
    core = lax.axis_index("core").astype(jnp.int32)
    for yl in range(YL):
        for zl in range(ZL):
            for m in range(ZH // 2):
                low = in_ref[yl * ZL + zl, core, 0, :, m * WIDE:(m + 1) * WIDE]
                high = in_ref[yl * ZL + zl, 1 - core, 0, :, m * WIDE:(m + 1) * WIDE]
                for h in range(2):
                    lanes = slice(h * BLOCK, (h + 1) * BLOCK)
                    at = ((yl * ZH + 2 * m + h) * ZL + zl) * WIDE
                    out_ref[0, :, at:at + WIDE] = jnp.concatenate(
                        [low[:, lanes], high[:, lanes]], axis=1
                    )


def body(
    trial_state,
    left_operators,
    right_operators,
    left_coupling,
    right_coupling,
    left_charge,
    right_charge,
):
    vectors, _, states = trial_state.shape
    smem = pl.BlockSpec(memory_space=pltpu.SMEM)
    vmem = pl.BlockSpec(memory_space=pltpu.VMEM)
    anywhere = pl.BlockSpec(memory_space=pl.ANY)
    params = pltpu.CompilerParams(vmem_limit_bytes=VMEM)
    small = pltpu.CompilerParams(vmem_limit_bytes=SMALL)

    wide = CORE * XROWS
    message = jax.ShapeDtypeStruct((YH * ZH, wide, WIDE), jnp.bfloat16)
    operator = jax.ShapeDtypeStruct((RROWS, WIDE), jnp.bfloat16)

    sent, left, right = pl.pallas_call(
        prepare_kernel,
        in_specs=[pl.BlockSpec(memory_space=pltpu.HBM)] * 5,
        out_specs=[anywhere, vmem, vmem],
        out_shape=[message, operator, operator],
        scratch_shapes=[
            pltpu.VMEM((YH * ZH, wide, WIDE), jnp.bfloat16),
            pltpu.VMEM((1, HERE), jnp.int32),
            pltpu.VMEM((1, HERE), jnp.int32),
            pltpu.VMEM(left_operators.shape, jnp.bfloat16),
            pltpu.VMEM(right_operators.shape, jnp.bfloat16),
            pltpu.VMEM((YH, HALF, states // YH), jnp.bfloat16),
            pltpu.SemaphoreType.DMA((2 * YH + 4,)),
        ],
        name="prepare_parts",
    )(
        left_coupling.reshape(1, HERE),
        right_coupling.reshape(1, HERE),
        left_operators,
        right_operators,
        trial_state,
    )
    got = lax.all_to_all(sent, FAR, 0, 0, tiled=True)

    swap = [(q * XDIM + x, x * XDIM + q) for q in range(YH) for x in range(XDIM)]
    left = lax.ppermute(left, ("yh", "op"), swap)

    across = [[(n, n ^ d) for n in range(XDIM)] for d in range(XDIM)]
    rights = [right] + [lax.ppermute(right, "op", across[d]) for d in (1, 2, 3)]

    plane = jax.ShapeDtypeStruct((ZH * wide, WIDE), jnp.bfloat16)
    *parts, left, right = pl.pallas_call(
        spread_kernel,
        in_specs=[vmem] * 6,
        out_specs=[vmem] * 6,
        out_shape=[plane] * XDIM
        + [
            jax.ShapeDtypeStruct((YH * ZH, RROWS, WIDE), jnp.bfloat16),
            jax.ShapeDtypeStruct((XDIM * RROWS, WIDE), jnp.bfloat16),
        ],
        compiler_params=small,
        name="spread_parts",
    )(got, left, *rights)
    left = lax.all_to_all(left, FAR, 0, 0, tiled=True)
    parts = parts[:1] + [lax.ppermute(parts[d], "op", across[d]) for d in (1, 2, 3)]

    rights = [right] + [
        lax.ppermute(right, NEAR, [(n, n ^ d) for n in range(YL * ZL)]) for d in (1, 2, 3)
    ]

    mine = jax.ShapeDtypeStruct((XDIM, ZH * (XROWS + RROWS), WIDE), jnp.bfloat16)
    near = jax.ShapeDtypeStruct((YL * ZL,) + right.shape, jnp.bfloat16)
    own, give, right = pl.pallas_call(
        core_kernel,
        in_specs=[vmem] * 9,
        out_specs=[vmem] * 3,
        out_shape=[mine, mine, near],
        compiler_params=small,
        name="sort_cores",
    )(left, *parts, *rights)
    other = lax.ppermute(give, "core", [(0, 1), (1, 0)])

    shared = [
        jax.ShapeDtypeStruct((TERMS, GROUP, GROUP), jnp.bfloat16),
        jax.ShapeDtypeStruct((4, CORE, vectors, BLOCK, GROUP), jnp.bfloat16),
    ]
    blocks = [
        pl.BlockSpec((4, 1, vectors, BLOCK, GROUP), lambda i, c=c: (0, c, 0, 0, 0))
        for c in range(CORE)
    ]
    keep = pl.BlockSpec(shared[0].shape, lambda v: (0, 0, 0))
    scratch = [
        pltpu.VMEM((GROUP, TERMS * GROUP), jnp.bfloat16),
        pltpu.VMEM((vectors * GROUP, TERMS * GROUP), jnp.bfloat16),
    ]
    inputs = [smem, smem] + [
        pl.BlockSpec(shape.shape, lambda v: (0, 0, 0)) for shape in (mine, near)
    ]
    partial, diagonal = pl.pallas_call(
        lambda *refs: sigma_kernel(0, *refs),
        grid=(1,),
        in_specs=inputs,
        out_specs=[blocks[0], keep],
        out_shape=shared[::-1],
        scratch_shapes=scratch,
        compiler_params=params,
        name="sigma_own",
    )(left_charge, right_charge, own, right)
    partial = pl.pallas_call(
        lambda lc, rc, got, *refs: sigma_kernel(1, lc, rc, got, None, *refs),
        grid=(1,),
        in_specs=inputs[:3] + [keep, anywhere],
        out_specs=blocks[1],
        out_shape=shared[1],
        scratch_shapes=scratch,
        input_output_aliases={4: 0},
        compiler_params=params,
        name="sigma_other",
    )(left_charge, right_charge, other, diagonal, partial)

    partial = lax.all_to_all(partial, NEAR, 0, 0, tiled=True)
    return pl.pallas_call(
        merge_kernel,
        grid=(vectors,),
        in_specs=[pl.BlockSpec((4, CORE, 1, BLOCK, GROUP), lambda v: (0, 0, v, 0, 0))],
        out_specs=pl.BlockSpec((1, BLOCK, 8 * GROUP), lambda v: (v, 0, 0)),
        out_shape=jax.ShapeDtypeStruct((vectors, BLOCK, 8 * GROUP), jnp.bfloat16),
        compiler_params=small,
        name="merge_sectors",
    )(partial)


def solution(mesh):
    fine = Mesh(mesh.devices.reshape(YH, YL, ZH, ZL, CORE, XDIM), SEC + ("op",))
    return jax.shard_map(
        body,
        mesh=fine,
        in_specs=(
            P(None, SEC, None),
            P("op", SEC, None),
            P("op", SEC, None),
            P("op", SEC),
            P("op", SEC),
            P(),
            P(),
        ),
        out_specs=P(None, SEC, "op"),
        check_vma=False,
    )
```

```python
import jax
import jax.numpy as jnp
import numpy as np
from jax import lax
from jax.experimental import pallas as pl
from jax.experimental.pallas import tpu as pltpu
from jax.sharding import Mesh, PartitionSpec as P

target_charge = 6
XDIM, YH, YL, ZH, ZL, CORE = 4, 4, 2, 4, 2, 2
SEC = ("yh", "yl", "zh", "zl", "core")
FAR = ("yh", "zh")
NEAR = ("yl", "zl")
NT = (((1,), (1,)), ((), ()))
BLOCK = 64
WIDE = 2 * BLOCK
HALF = BLOCK // 2
GROUP = 4 * BLOCK
TERMS = 24
HERE = TERMS // XDIM
PAIRS = HERE // 2
XROWS = 2 * HALF
RROWS = PAIRS * BLOCK
FROM = ZH * CORE
VMEM = 24 * 1024 * 1024
SMALL = 8 * 1024 * 1024


def swap_halves(piece):
    return jnp.concatenate([piece[:, BLOCK:], piece[:, :BLOCK]], axis=1)


def placed(piece, second, to_second):
    lane = lax.broadcasted_iota(jnp.int32, piece.shape, 1)
    moved = piece if second == to_second else swap_halves(piece)
    keep = (lane >= BLOCK) if to_second else (lane < BLOCK)
    return jnp.where(keep, moved, jnp.zeros_like(moved))


def across(core):
    return 0, 1 + 2 * core, 2, 3 - 2 * core


def around(core):
    return 0, 1 + core, 2 - core, 3


def place():
    return [lax.axis_index(n).astype(jnp.int32) for n in ("op",) + SEC]


def turned(core, first, second, size=4):
    return jnp.where(core == 0, first * size + second, second * size + first)


def prepare_kernel(
    lc_in, rc_in, left_in, right_in, x_ref, out_ref, lout_ref, rout_ref,
    sent_ref, lc_ref, rc_ref, left_ref, right_ref, rows_ref, sems,
):
    plane = lax.axis_index("op").astype(jnp.int32)
    core = lax.axis_index("core").astype(jnp.int32)
    lanes_of = rows_ref.shape[2]
    copies = []

    def copy(source, to):
        copies.append(pltpu.make_async_copy(source, to, sems.at[len(copies)]))
        copies[-1].start()

    for yh in range(YH):
        source = x_ref.at[
            plane // 2,
            pl.ds(pl.multiple_of(lax.rem(plane, 2) * HALF, HALF), HALF),
            pl.ds(yh * lanes_of, lanes_of),
        ]
        copy(source, rows_ref.at[yh])
    copy(left_in, left_ref)
    copy(right_in, right_ref)
    copy(lc_in, lc_ref)
    copy(rc_in, rc_ref)
    for yh in range(YH):
        copies[yh].wait()
        for yl in range(YL):
            for zh in range(ZH):
                at = (yl * ZH + zh) * ZL
                first = rows_ref[yh, :, at * WIDE:(at + 1) * WIDE]
                second = rows_ref[yh, :, (at + 1) * WIDE:(at + 2) * WIDE]
                for c in range(CORE):
                    lanes = slice(c * BLOCK, (c + 1) * BLOCK)
                    rows = slice(c * XROWS + yl * HALF, c * XROWS + (yl + 1) * HALF)
                    sent_ref[yh * ZH + zh, rows, :] = jnp.concatenate(
                        [first[:, lanes], second[:, lanes]], axis=1
                    )
        for zh in range(ZH):
            copy(sent_ref.at[yh * ZH + zh], out_ref.at[turned(core, yh, zh)])
    for n, (c_ref, in_ref, to_ref) in enumerate(
        ((lc_ref, left_ref, lout_ref), (rc_ref, right_ref, rout_ref))
    ):
        copies[YH + n].wait()
        copies[YH + 2 + n].wait()
        scale = c_ref[...].astype(jnp.float32)
        for p in range(PAIRS):
            both = []
            for t in (2 * p, 2 * p + 1):
                scaled = in_ref[t].astype(jnp.float32) * scale[:, t:t + 1]
                both.append(scaled.astype(jnp.bfloat16))
            to_ref[p * BLOCK:(p + 1) * BLOCK, :] = jnp.concatenate(both, axis=1)
    for done in copies[YH + 4:]:
        done.wait()


def spread_kernel(
    got_ref, left_ref, r0_ref, ra_ref, rb_ref, rc_ref, p0_ref, pa_ref, pb_ref, pc_ref, sent_ref
):
    plane = lax.axis_index("op").astype(jnp.int32)
    core = lax.axis_index("core").astype(jnp.int32)
    wide = CORE * XROWS
    for ref, d in zip((p0_ref, pa_ref, pb_ref, pc_ref), across(core)):
        to = jnp.bitwise_xor(plane, d)
        for z in range(ZH):
            ref[z * wide:(z + 1) * wide, :] = got_ref[turned(core, to, z)]
        for right_ref, e in zip((r0_ref, ra_ref, rb_ref, rc_ref), around(core)):
            rows = pl.ds(pl.multiple_of(ZH * wide + e * RROWS, BLOCK), RROWS)
            ref[rows, :] = right_ref[...]
    for to in range(YH * ZH):
        sent_ref[to] = left_ref[...]


def core_kernel(left_ref, p0_ref, pa_ref, pb_ref, pc_ref, own_ref, give_ref, near_ref):
    x_at, _, yl_at, _, zl_at, core = place()
    for ref, d in zip((p0_ref, pa_ref, pb_ref, pc_ref), across(core)):
        x = jnp.bitwise_xor(x_at, d)
        for z in range(ZH):
            rows = slice(z * XROWS, (z + 1) * XROWS)
            for to_ref, c in ((own_ref, core), (give_ref, 1 - core)):
                at = pl.multiple_of((z * CORE + c) * XROWS, XROWS)
                to_ref[x, rows, :] = ref[pl.ds(at, XROWS), :]
        rows = pl.ds(pl.multiple_of(x * RROWS, BLOCK), RROWS)
        for e in range(YL * ZL):
            at = FROM * XROWS + e * RROWS
            near_ref[jnp.bitwise_xor(yl_at * ZL + zl_at, e), rows, :] = ref[at:at + RROWS, :]
    for x in range(XDIM):
        for z in range(ZH):
            rows = slice(ZH * XROWS + z * RROWS, ZH * XROWS + (z + 1) * RROWS)
            left = left_ref[turned(core, x, z)]
            own_ref[x, rows, :] = left
            give_ref[x, rows, :] = left


def build_right(near_ref, right_ref):
    zeros = jnp.zeros((BLOCK, WIDE), jnp.bfloat16)
    for b in range(4):
        rows = slice(b * BLOCK, (b + 1) * BLOCK)
        used = slice((b // 2) * WIDE, (b // 2 + 1) * WIDE)
        unused = slice((1 - b // 2) * WIDE, (2 - b // 2) * WIDE)
        for d in range(XDIM):
            first = d * HERE
            for p in range(PAIRS):
                at = d * RROWS + p * BLOCK
                piece = near_ref[b, at:at + BLOCK, :]
                for s in range(2):
                    right_ref[first + 2 * p + s, rows, used] = placed(piece, s, b % 2)
                    right_ref[first + 2 * p + s, rows, unused] = zeros


def build_left(got_ref, left_ref):
    zeros = jnp.zeros((BLOCK, WIDE), jnp.bfloat16)
    for x in range(XDIM):
        for z in range(ZH):
            rows = slice(z * BLOCK, (z + 1) * BLOCK)
            for p in range(PAIRS):
                at = ZH * XROWS + z * RROWS + p * BLOCK
                piece = got_ref[x, at:at + BLOCK, :]
                for s in range(2):
                    at = (x * HERE + 2 * p + s) * GROUP
                    used, unused = at + (z // 2) * WIDE, at + (1 - z // 2) * WIDE
                    left_ref[rows, used:used + WIDE] = placed(piece, s, z % 2)
                    left_ref[rows, unused:unused + WIDE] = zeros


def sigma_kernel(c, lcharge_ref, rcharge_ref, got_ref, near_ref, *refs):
    if c == 0:
        out_ref, right_ref, left_ref, half_ref = refs
    else:
        right_ref, _, out_ref, left_ref, half_ref = refs
    x_at, yh_at, yl_at, zh_at, zl_at, core = place()
    if c == 0:
        build_right(near_ref, right_ref)
    vectors = half_ref.shape[0] // GROUP
    for v in range(vectors):
        rows = []
        for z in range(ZH):
            for h in range(2):
                piece = got_ref[v * 2 + h, z * XROWS:(z + 1) * XROWS, :]
                rows.append(jnp.concatenate([piece[:HALF], piece[HALF:]], axis=1))
        state = jnp.concatenate(rows, axis=0)
        for t in range(TERMS):
            out = lax.dot_general(right_ref[t], state, NT, preferred_element_type=jnp.float32)
            half_ref[v * GROUP:(v + 1) * GROUP, t * GROUP:(t + 1) * GROUP] = out.astype(
                half_ref.dtype
            )
    build_left(got_ref, left_ref)
    out = lax.dot_general(half_ref[...], left_ref[...], NT, preferred_element_type=jnp.float32)

    lane = lax.broadcasted_iota(jnp.int32, (1, GROUP), 1) // BLOCK
    charge = jnp.zeros((1, GROUP), jnp.int32)
    for z in range(ZH):
        sector = (((x_at * YL + yl_at) * ZH + z) * ZL + zl_at) * CORE + jnp.bitwise_xor(core, c)
        charge = jnp.where(lane == z, lcharge_ref[sector], charge)
    for b in range(4):
        sector = (((yh_at * YL + b // 2) * ZH + zh_at) * ZL + b % 2) * CORE + core
        allowed = jnp.abs(charge + rcharge_ref[sector] - target_charge) <= 1
        for v in range(vectors):
            at = v * GROUP + b * BLOCK
            block = out[at:at + BLOCK]
            out_ref[turned(core, b // 2, b % 2, 2), 0, v] = jnp.where(allowed, block, jnp.zeros_like(block)).astype(
                out_ref.dtype
            )


def merge_kernel(in_ref, out_ref):
    core = lax.axis_index("core").astype(jnp.int32)
    for yl in range(YL):
        for zl in range(ZL):
            for m in range(ZH // 2):
                low = in_ref[turned(core, yl, zl, 2), core, 0, :, m * WIDE:(m + 1) * WIDE]
                high = in_ref[turned(core, yl, zl, 2), 1 - core, 0, :, m * WIDE:(m + 1) * WIDE]
                for h in range(2):
                    lanes = slice(h * BLOCK, (h + 1) * BLOCK)
                    at = ((yl * ZH + 2 * m + h) * ZL + zl) * WIDE
                    out_ref[0, :, at:at + WIDE] = jnp.concatenate(
                        [low[:, lanes], high[:, lanes]], axis=1
                    )


def exchange(array, ids, axes):
    ids = np.moveaxis(ids, [SEC.index(a) for a in axes], [-2, -1])
    at = [a for a in SEC if a not in axes].index("core")
    groups = []
    for index in np.ndindex(*ids.shape[:-2]):
        group = ids[index] if index[at] == 0 else ids[index].T
        groups.append([int(n) for n in group.reshape(-1)])
    return lax.all_to_all(array, SEC + ("op",), 0, 0, tiled=True, axis_index_groups=groups)


def partners(axis_of_core, steps):
    pairs = []
    for core in range(CORE):
        for n in range(4):
            to = n ^ steps[core]
            if axis_of_core == 0:
                pairs.append((core * 4 + n, core * 4 + to))
            else:
                pairs.append((n * CORE + core, to * CORE + core))
    return pairs


def body(
    trial_state,
    left_operators,
    right_operators,
    left_coupling,
    right_coupling,
    left_charge,
    right_charge,
):
    vectors, _, states = trial_state.shape
    ids = np.arange(YH * YL * ZH * ZL * CORE * XDIM).reshape(YH, YL, ZH, ZL, CORE, XDIM)
    smem = pl.BlockSpec(memory_space=pltpu.SMEM)
    vmem = pl.BlockSpec(memory_space=pltpu.VMEM)
    anywhere = pl.BlockSpec(memory_space=pl.ANY)
    params = pltpu.CompilerParams(vmem_limit_bytes=VMEM)
    small = pltpu.CompilerParams(vmem_limit_bytes=SMALL)

    wide = CORE * XROWS
    message = jax.ShapeDtypeStruct((YH * ZH, wide, WIDE), jnp.bfloat16)
    operator = jax.ShapeDtypeStruct((RROWS, WIDE), jnp.bfloat16)

    sent, left, right = pl.pallas_call(
        prepare_kernel,
        in_specs=[pl.BlockSpec(memory_space=pltpu.HBM)] * 5,
        out_specs=[anywhere, vmem, vmem],
        out_shape=[message, operator, operator],
        scratch_shapes=[
            pltpu.VMEM((YH * ZH, wide, WIDE), jnp.bfloat16),
            pltpu.VMEM((1, HERE), jnp.int32),
            pltpu.VMEM((1, HERE), jnp.int32),
            pltpu.VMEM(left_operators.shape, jnp.bfloat16),
            pltpu.VMEM(right_operators.shape, jnp.bfloat16),
            pltpu.VMEM((YH, HALF, states // YH), jnp.bfloat16),
            pltpu.SemaphoreType.DMA((YH + 4 + YH * ZH,)),
        ],
        name="prepare_parts",
    )(
        left_coupling.reshape(1, HERE),
        right_coupling.reshape(1, HERE),
        left_operators,
        right_operators,
        trial_state,
    )
    got = exchange(sent, ids, FAR)

    swap = [(q * XDIM + x, x * XDIM + q) for q in range(YH) for x in range(XDIM)]
    left = lax.ppermute(left, ("yh", "op"), swap)

    rights = [right] + [
        lax.ppermute(right, NEAR + ("core",), partners(1, [around(c)[n] for c in range(CORE)]))
        for n in (1, 2, 3)
    ]

    pack = jax.ShapeDtypeStruct((ZH * wide + YL * ZL * RROWS, WIDE), jnp.bfloat16)
    *packs, left = pl.pallas_call(
        spread_kernel,
        in_specs=[vmem] * 6,
        out_specs=[vmem] * 5,
        out_shape=[pack] * XDIM + [jax.ShapeDtypeStruct((YH * ZH, RROWS, WIDE), jnp.bfloat16)],
        compiler_params=small,
        name="spread_parts",
    )(got, left, *rights)
    left = exchange(left, ids, FAR)
    packs = packs[:1] + [
        lax.ppermute(packs[n], ("core", "op"), partners(0, [across(c)[n] for c in range(CORE)]))
        for n in (1, 2, 3)
    ]

    mine = jax.ShapeDtypeStruct((XDIM, ZH * (XROWS + RROWS), WIDE), jnp.bfloat16)
    near = jax.ShapeDtypeStruct((YL * ZL, XDIM * RROWS, WIDE), jnp.bfloat16)
    own, give, right = pl.pallas_call(
        core_kernel,
        in_specs=[vmem] * 5,
        out_specs=[vmem] * 3,
        out_shape=[mine, mine, near],
        compiler_params=small,
        name="sort_cores",
    )(left, *packs)
    other = lax.ppermute(give, "core", [(0, 1), (1, 0)])

    shared = [
        jax.ShapeDtypeStruct((TERMS, GROUP, GROUP), jnp.bfloat16),
        jax.ShapeDtypeStruct((4, CORE, vectors, BLOCK, GROUP), jnp.bfloat16),
    ]
    blocks = [
        pl.BlockSpec((4, 1, vectors, BLOCK, GROUP), lambda i, c=c: (0, c, 0, 0, 0))
        for c in range(CORE)
    ]
    keep = pl.BlockSpec(shared[0].shape, lambda v: (0, 0, 0))
    scratch = [
        pltpu.VMEM((GROUP, TERMS * GROUP), jnp.bfloat16),
        pltpu.VMEM((vectors * GROUP, TERMS * GROUP), jnp.bfloat16),
    ]
    inputs = [smem, smem] + [
        pl.BlockSpec(shape.shape, lambda v: (0, 0, 0)) for shape in (mine, near)
    ]
    partial, diagonal = pl.pallas_call(
        lambda *refs: sigma_kernel(0, *refs),
        grid=(1,),
        in_specs=inputs,
        out_specs=[blocks[0], keep],
        out_shape=shared[::-1],
        scratch_shapes=scratch,
        compiler_params=params,
        name="sigma_own",
    )(left_charge, right_charge, own, right)
    partial = pl.pallas_call(
        lambda lc, rc, got, *refs: sigma_kernel(1, lc, rc, got, None, *refs),
        grid=(1,),
        in_specs=inputs[:3] + [keep, anywhere],
        out_specs=blocks[1],
        out_shape=shared[1],
        scratch_shapes=scratch,
        input_output_aliases={4: 0},
        compiler_params=params,
        name="sigma_other",
    )(left_charge, right_charge, other, diagonal, partial)

    partial = exchange(partial, ids, NEAR)
    return pl.pallas_call(
        merge_kernel,
        grid=(vectors,),
        in_specs=[pl.BlockSpec((4, CORE, 1, BLOCK, GROUP), lambda v: (0, 0, v, 0, 0))],
        out_specs=pl.BlockSpec((1, BLOCK, 8 * GROUP), lambda v: (v, 0, 0)),
        out_shape=jax.ShapeDtypeStruct((vectors, BLOCK, 8 * GROUP), jnp.bfloat16),
        compiler_params=small,
        name="merge_sectors",
    )(partial)


def solution(mesh):
    fine = Mesh(mesh.devices.reshape(YH, YL, ZH, ZL, CORE, XDIM), SEC + ("op",))
    return jax.shard_map(
        body,
        mesh=fine,
        in_specs=(
            P(None, SEC, None),
            P("op", SEC, None),
            P("op", SEC, None),
            P("op", SEC),
            P("op", SEC),
            P(),
            P(),
        ),
        out_specs=P(None, SEC, "op"),
        check_vma=False,
    )
```

```python
import jax
import jax.numpy as jnp
import numpy as np
from jax import lax
from jax.experimental import pallas as pl
from jax.experimental.pallas import tpu as pltpu
from jax.sharding import Mesh, PartitionSpec as P

target_charge = 6
XDIM, YH, YL, ZH, ZL, CORE = 4, 4, 2, 4, 2, 2
SEC = ("yh", "yl", "zh", "zl", "core")
FAR = ("yh", "zh")
NEAR = ("yl", "zl")
NT = (((1,), (1,)), ((), ()))
BLOCK = 64
WIDE = 2 * BLOCK
HALF = BLOCK // 2
GROUP = 4 * BLOCK
TERMS = 24
HERE = TERMS // XDIM
PAIRS = HERE // 2
XROWS = 2 * HALF
RROWS = PAIRS * BLOCK
FROM = ZH * CORE
VMEM = 24 * 1024 * 1024
SMALL = 8 * 1024 * 1024


def swap_halves(piece):
    return jnp.concatenate([piece[:, BLOCK:], piece[:, :BLOCK]], axis=1)


def placed(piece, second, to_second):
    lane = lax.broadcasted_iota(jnp.int32, piece.shape, 1)
    moved = piece if second == to_second else swap_halves(piece)
    keep = (lane >= BLOCK) if to_second else (lane < BLOCK)
    return jnp.where(keep, moved, jnp.zeros_like(moved))


def across(core):
    return 0, 1 + 2 * core, 2, 3 - 2 * core


def around(core):
    return 0, 1 + core, 2 - core, 3


def place():
    return [lax.axis_index(n).astype(jnp.int32) for n in ("op",) + SEC]


def turned(core, first, second, size=4):
    return jnp.where(core == 0, first * size + second, second * size + first)


def prepare_kernel(
    lc_in, rc_in, left_in, right_in, x_ref, out_ref, lout_ref, rout_ref,
    sent_ref, lc_ref, rc_ref, left_ref, right_ref, rows_ref, sems,
):
    plane = lax.axis_index("op").astype(jnp.int32)
    core = lax.axis_index("core").astype(jnp.int32)
    lanes_of = rows_ref.shape[2]
    copies = []

    def copy(source, to):
        copies.append(pltpu.make_async_copy(source, to, sems.at[len(copies)]))
        copies[-1].start()

    for yh in range(YH):
        source = x_ref.at[
            plane // 2,
            pl.ds(pl.multiple_of(lax.rem(plane, 2) * HALF, HALF), HALF),
            pl.ds(yh * lanes_of, lanes_of),
        ]
        copy(source, rows_ref.at[yh])
    copy(left_in, left_ref)
    copy(right_in, right_ref)
    copy(lc_in, lc_ref)
    copy(rc_in, rc_ref)
    for yh in range(YH):
        copies[yh].wait()
        for yl in range(YL):
            for zh in range(ZH):
                at = (yl * ZH + zh) * ZL
                first = rows_ref[yh, :, at * WIDE:(at + 1) * WIDE]
                second = rows_ref[yh, :, (at + 1) * WIDE:(at + 2) * WIDE]
                for c in range(CORE):
                    lanes = slice(c * BLOCK, (c + 1) * BLOCK)
                    rows = slice(c * XROWS + yl * HALF, c * XROWS + (yl + 1) * HALF)
                    sent_ref[yh * ZH + zh, rows, :] = jnp.concatenate(
                        [first[:, lanes], second[:, lanes]], axis=1
                    )
        for zh in range(ZH):
            copy(sent_ref.at[yh * ZH + zh], out_ref.at[turned(core, yh, zh)])
    for n, (c_ref, in_ref, to_ref) in enumerate(
        ((lc_ref, left_ref, lout_ref), (rc_ref, right_ref, rout_ref))
    ):
        copies[YH + n].wait()
        copies[YH + 2 + n].wait()
        scale = c_ref[...].astype(jnp.float32)
        for p in range(PAIRS):
            both = []
            for t in (2 * p, 2 * p + 1):
                scaled = in_ref[t].astype(jnp.float32) * scale[:, t:t + 1]
                both.append(scaled.astype(jnp.bfloat16))
            to_ref[p * BLOCK:(p + 1) * BLOCK, :] = jnp.concatenate(both, axis=1)
    for done in copies[YH + 4:]:
        done.wait()


def spread_kernel(
    got_ref, left_ref, r0_ref, ra_ref, rb_ref, rc_ref, p0_ref, pa_ref, pb_ref, pc_ref, sent_ref
):
    plane = lax.axis_index("op").astype(jnp.int32)
    core = lax.axis_index("core").astype(jnp.int32)
    wide = CORE * XROWS
    for ref, d in zip((p0_ref, pa_ref, pb_ref, pc_ref), across(core)):
        to = jnp.bitwise_xor(plane, d)
        for z in range(ZH):
            ref[z * wide:(z + 1) * wide, :] = got_ref[turned(core, to, z)]
        for right_ref, e in zip((r0_ref, ra_ref, rb_ref, rc_ref), around(core)):
            rows = pl.ds(pl.multiple_of(ZH * wide + e * RROWS, BLOCK), RROWS)
            ref[rows, :] = right_ref[...]
    for to in range(YH * ZH):
        sent_ref[to] = left_ref[...]


def core_kernel(left_ref, p0_ref, pa_ref, pb_ref, pc_ref, own_ref, give_ref, near_ref):
    x_at, _, yl_at, _, zl_at, core = place()
    for ref, d in zip((p0_ref, pa_ref, pb_ref, pc_ref), across(core)):
        x = jnp.bitwise_xor(x_at, d)
        for z in range(ZH):
            rows = slice(z * XROWS, (z + 1) * XROWS)
            for to_ref, c in ((own_ref, core), (give_ref, 1 - core)):
                at = pl.multiple_of((z * CORE + c) * XROWS, XROWS)
                to_ref[x, rows, :] = ref[pl.ds(at, XROWS), :]
        rows = pl.ds(pl.multiple_of(x * RROWS, BLOCK), RROWS)
        for e in range(YL * ZL):
            at = FROM * XROWS + e * RROWS
            near_ref[jnp.bitwise_xor(yl_at * ZL + zl_at, e), rows, :] = ref[at:at + RROWS, :]
    for x in range(XDIM):
        for z in range(ZH):
            rows = slice(ZH * XROWS + z * RROWS, ZH * XROWS + (z + 1) * RROWS)
            n = x * ZH + z
            left = left_ref[jnp.where(core == 0, n, YH * ZH - 1 - n)]
            own_ref[x, rows, :] = left
            give_ref[x, rows, :] = left


def build_right(near_ref, right_ref):
    zeros = jnp.zeros((BLOCK, WIDE), jnp.bfloat16)
    for b in range(4):
        rows = slice(b * BLOCK, (b + 1) * BLOCK)
        used = slice((b // 2) * WIDE, (b // 2 + 1) * WIDE)
        unused = slice((1 - b // 2) * WIDE, (2 - b // 2) * WIDE)
        for d in range(XDIM):
            first = d * HERE
            for p in range(PAIRS):
                at = d * RROWS + p * BLOCK
                piece = near_ref[b, at:at + BLOCK, :]
                for s in range(2):
                    right_ref[first + 2 * p + s, rows, used] = placed(piece, s, b % 2)
                    right_ref[first + 2 * p + s, rows, unused] = zeros


def build_left(got_ref, left_ref):
    zeros = jnp.zeros((BLOCK, WIDE), jnp.bfloat16)
    for x in range(XDIM):
        for z in range(ZH):
            rows = slice(z * BLOCK, (z + 1) * BLOCK)
            for p in range(PAIRS):
                at = ZH * XROWS + z * RROWS + p * BLOCK
                piece = got_ref[x, at:at + BLOCK, :]
                for s in range(2):
                    at = (x * HERE + 2 * p + s) * GROUP
                    used, unused = at + (z // 2) * WIDE, at + (1 - z // 2) * WIDE
                    left_ref[rows, used:used + WIDE] = placed(piece, s, z % 2)
                    left_ref[rows, unused:unused + WIDE] = zeros


def sigma_kernel(c, lcharge_ref, rcharge_ref, got_ref, near_ref, *refs):
    if c == 0:
        out_ref, right_ref, left_ref, half_ref = refs
    else:
        right_ref, _, out_ref, left_ref, half_ref = refs
    x_at, yh_at, yl_at, zh_at, zl_at, core = place()
    if c == 0:
        build_right(near_ref, right_ref)
    vectors = half_ref.shape[0] // GROUP
    for v in range(vectors):
        rows = []
        for z in range(ZH):
            for h in range(2):
                piece = got_ref[v * 2 + h, z * XROWS:(z + 1) * XROWS, :]
                rows.append(jnp.concatenate([piece[:HALF], piece[HALF:]], axis=1))
        state = jnp.concatenate(rows, axis=0)
        for t in range(TERMS):
            out = lax.dot_general(right_ref[t], state, NT, preferred_element_type=jnp.float32)
            half_ref[v * GROUP:(v + 1) * GROUP, t * GROUP:(t + 1) * GROUP] = out.astype(
                half_ref.dtype
            )
    build_left(got_ref, left_ref)
    out = lax.dot_general(half_ref[...], left_ref[...], NT, preferred_element_type=jnp.float32)

    lane = lax.broadcasted_iota(jnp.int32, (1, GROUP), 1) // BLOCK
    charge = jnp.zeros((1, GROUP), jnp.int32)
    for z in range(ZH):
        sector = (((x_at * YL + yl_at) * ZH + z) * ZL + zl_at) * CORE + jnp.bitwise_xor(core, c)
        charge = jnp.where(lane == z, lcharge_ref[sector], charge)
    for b in range(4):
        sector = (((yh_at * YL + b // 2) * ZH + zh_at) * ZL + b % 2) * CORE + core
        allowed = jnp.abs(charge + rcharge_ref[sector] - target_charge) <= 1
        for v in range(vectors):
            at = v * GROUP + b * BLOCK
            block = out[at:at + BLOCK]
            out_ref[turned(core, b // 2, b % 2, 2), 0, v] = jnp.where(allowed, block, jnp.zeros_like(block)).astype(
                out_ref.dtype
            )


def merge_kernel(in_ref, out_ref):
    core = lax.axis_index("core").astype(jnp.int32)
    for yl in range(YL):
        for zl in range(ZL):
            for m in range(ZH // 2):
                low = in_ref[turned(core, yl, zl, 2), core, 0, :, m * WIDE:(m + 1) * WIDE]
                high = in_ref[turned(core, yl, zl, 2), 1 - core, 0, :, m * WIDE:(m + 1) * WIDE]
                for h in range(2):
                    lanes = slice(h * BLOCK, (h + 1) * BLOCK)
                    at = ((yl * ZH + 2 * m + h) * ZL + zl) * WIDE
                    out_ref[0, :, at:at + WIDE] = jnp.concatenate(
                        [low[:, lanes], high[:, lanes]], axis=1
                    )


def exchange(array, ids, axes, backwards=False):
    ids = np.moveaxis(ids, [SEC.index(a) for a in axes], [-2, -1])
    at = [a for a in SEC if a not in axes].index("core")
    groups = []
    for index in np.ndindex(*ids.shape[:-2]):
        group = ids[index]
        if index[at] == 1:
            group = np.flip(group) if backwards else group.T
        groups.append([int(n) for n in group.reshape(-1)])
    return lax.all_to_all(array, SEC + ("op",), 0, 0, tiled=True, axis_index_groups=groups)


def partners(axis_of_core, steps):
    pairs = []
    for core in range(CORE):
        for n in range(4):
            to = n ^ steps[core]
            if axis_of_core == 0:
                pairs.append((core * 4 + n, core * 4 + to))
            else:
                pairs.append((n * CORE + core, to * CORE + core))
    return pairs


def body(
    trial_state,
    left_operators,
    right_operators,
    left_coupling,
    right_coupling,
    left_charge,
    right_charge,
):
    vectors, _, states = trial_state.shape
    ids = np.arange(YH * YL * ZH * ZL * CORE * XDIM).reshape(YH, YL, ZH, ZL, CORE, XDIM)
    smem = pl.BlockSpec(memory_space=pltpu.SMEM)
    vmem = pl.BlockSpec(memory_space=pltpu.VMEM)
    anywhere = pl.BlockSpec(memory_space=pl.ANY)
    params = pltpu.CompilerParams(vmem_limit_bytes=VMEM)
    small = pltpu.CompilerParams(vmem_limit_bytes=SMALL)

    wide = CORE * XROWS
    message = jax.ShapeDtypeStruct((YH * ZH, wide, WIDE), jnp.bfloat16)
    operator = jax.ShapeDtypeStruct((RROWS, WIDE), jnp.bfloat16)

    sent, left, right = pl.pallas_call(
        prepare_kernel,
        in_specs=[pl.BlockSpec(memory_space=pltpu.HBM)] * 5,
        out_specs=[anywhere, vmem, vmem],
        out_shape=[message, operator, operator],
        scratch_shapes=[
            pltpu.VMEM((YH * ZH, wide, WIDE), jnp.bfloat16),
            pltpu.VMEM((1, HERE), jnp.int32),
            pltpu.VMEM((1, HERE), jnp.int32),
            pltpu.VMEM(left_operators.shape, jnp.bfloat16),
            pltpu.VMEM(right_operators.shape, jnp.bfloat16),
            pltpu.VMEM((YH, HALF, states // YH), jnp.bfloat16),
            pltpu.SemaphoreType.DMA((YH + 4 + YH * ZH,)),
        ],
        name="prepare_parts",
    )(
        left_coupling.reshape(1, HERE),
        right_coupling.reshape(1, HERE),
        left_operators,
        right_operators,
        trial_state,
    )
    got = exchange(sent, ids, FAR)

    swap = [(q * XDIM + x, x * XDIM + q) for q in range(YH) for x in range(XDIM)]
    left = lax.ppermute(left, ("yh", "op"), swap)

    rights = [right] + [
        lax.ppermute(right, NEAR + ("core",), partners(1, [around(c)[n] for c in range(CORE)]))
        for n in (1, 2, 3)
    ]

    pack = jax.ShapeDtypeStruct((ZH * wide + YL * ZL * RROWS, WIDE), jnp.bfloat16)
    *packs, left = pl.pallas_call(
        spread_kernel,
        in_specs=[vmem] * 6,
        out_specs=[vmem] * 5,
        out_shape=[pack] * XDIM + [jax.ShapeDtypeStruct((YH * ZH, RROWS, WIDE), jnp.bfloat16)],
        compiler_params=small,
        name="spread_parts",
    )(got, left, *rights)
    left = exchange(left, ids, FAR, backwards=True)
    packs = packs[:1] + [
        lax.ppermute(packs[n], ("core", "op"), partners(0, [across(c)[n] for c in range(CORE)]))
        for n in (1, 2, 3)
    ]

    mine = jax.ShapeDtypeStruct((XDIM, ZH * (XROWS + RROWS), WIDE), jnp.bfloat16)
    near = jax.ShapeDtypeStruct((YL * ZL, XDIM * RROWS, WIDE), jnp.bfloat16)
    own, give, right = pl.pallas_call(
        core_kernel,
        in_specs=[vmem] * 5,
        out_specs=[vmem] * 3,
        out_shape=[mine, mine, near],
        compiler_params=small,
        name="sort_cores",
    )(left, *packs)
    other = lax.ppermute(give, "core", [(0, 1), (1, 0)])

    shared = [
        jax.ShapeDtypeStruct((TERMS, GROUP, GROUP), jnp.bfloat16),
        jax.ShapeDtypeStruct((4, CORE, vectors, BLOCK, GROUP), jnp.bfloat16),
    ]
    blocks = [
        pl.BlockSpec((4, 1, vectors, BLOCK, GROUP), lambda i, c=c: (0, c, 0, 0, 0))
        for c in range(CORE)
    ]
    keep = pl.BlockSpec(shared[0].shape, lambda v: (0, 0, 0))
    scratch = [
        pltpu.VMEM((GROUP, TERMS * GROUP), jnp.bfloat16),
        pltpu.VMEM((vectors * GROUP, TERMS * GROUP), jnp.bfloat16),
    ]
    inputs = [smem, smem] + [
        pl.BlockSpec(shape.shape, lambda v: (0, 0, 0)) for shape in (mine, near)
    ]
    partial, diagonal = pl.pallas_call(
        lambda *refs: sigma_kernel(0, *refs),
        grid=(1,),
        in_specs=inputs,
        out_specs=[blocks[0], keep],
        out_shape=shared[::-1],
        scratch_shapes=scratch,
        compiler_params=params,
        name="sigma_own",
    )(left_charge, right_charge, own, right)
    partial = pl.pallas_call(
        lambda lc, rc, got, *refs: sigma_kernel(1, lc, rc, got, None, *refs),
        grid=(1,),
        in_specs=inputs[:3] + [keep, anywhere],
        out_specs=blocks[1],
        out_shape=shared[1],
        scratch_shapes=scratch,
        input_output_aliases={4: 0},
        compiler_params=params,
        name="sigma_other",
    )(left_charge, right_charge, other, diagonal, partial)

    partial = exchange(partial, ids, NEAR)
    return pl.pallas_call(
        merge_kernel,
        grid=(vectors,),
        in_specs=[pl.BlockSpec((4, CORE, 1, BLOCK, GROUP), lambda v: (0, 0, v, 0, 0))],
        out_specs=pl.BlockSpec((1, BLOCK, 8 * GROUP), lambda v: (v, 0, 0)),
        out_shape=jax.ShapeDtypeStruct((vectors, BLOCK, 8 * GROUP), jnp.bfloat16),
        compiler_params=small,
        name="merge_sectors",
    )(partial)


def solution(mesh):
    fine = Mesh(mesh.devices.reshape(YH, YL, ZH, ZL, CORE, XDIM), SEC + ("op",))
    return jax.shard_map(
        body,
        mesh=fine,
        in_specs=(
            P(None, SEC, None),
            P("op", SEC, None),
            P("op", SEC, None),
            P("op", SEC),
            P("op", SEC),
            P(),
            P(),
        ),
        out_specs=P(None, SEC, "op"),
        check_vma=False,
    )
```

```python
import jax
import jax.numpy as jnp
import numpy as np
from jax import lax
from jax.experimental import pallas as pl
from jax.experimental.pallas import tpu as pltpu
from jax.sharding import Mesh, PartitionSpec as P

target_charge = 6
XDIM, YH, YL, ZH, ZL, CORE = 4, 4, 2, 4, 2, 2
SEC = ("yh", "yl", "zh", "zl", "core")
FAR = ("yh", "zh")
NEAR = ("yl", "zl")
X_ORDER, L_ORDER, OUT_ORDER = "backwards", "both", "backwards"
NT = (((1,), (1,)), ((), ()))
BLOCK = 64
WIDE = 2 * BLOCK
HALF = BLOCK // 2
GROUP = 4 * BLOCK
TERMS = 24
HERE = TERMS // XDIM
PAIRS = HERE // 2
XROWS = 2 * HALF
RROWS = PAIRS * BLOCK
FROM = ZH * CORE
VMEM = 24 * 1024 * 1024
SMALL = 8 * 1024 * 1024


def swap_halves(piece):
    return jnp.concatenate([piece[:, BLOCK:], piece[:, :BLOCK]], axis=1)


def placed(piece, second, to_second):
    lane = lax.broadcasted_iota(jnp.int32, piece.shape, 1)
    moved = piece if second == to_second else swap_halves(piece)
    keep = (lane >= BLOCK) if to_second else (lane < BLOCK)
    return jnp.where(keep, moved, jnp.zeros_like(moved))


def across(core):
    return 0, 1 + 2 * core, 2, 3 - 2 * core


def around(core):
    return 0, 1 + core, 2 - core, 3


def place():
    return [lax.axis_index(n).astype(jnp.int32) for n in ("op",) + SEC]


def turned(core, first, second, size, order):
    n, turn = first * size + second, second * size + first
    last = size * size - 1
    return jnp.where(core == 0, n, {"columns": turn, "backwards": last - n, "both": last - turn}[order])


def prepare_kernel(
    lc_in, rc_in, left_in, right_in, x_ref, out_ref, lout_ref, rout_ref,
    sent_ref, lc_ref, rc_ref, left_ref, right_ref, rows_ref, sems,
):
    plane = lax.axis_index("op").astype(jnp.int32)
    core = lax.axis_index("core").astype(jnp.int32)
    lanes_of = rows_ref.shape[2]
    copies = []

    def copy(source, to):
        copies.append(pltpu.make_async_copy(source, to, sems.at[len(copies)]))
        copies[-1].start()

    for yh in range(YH):
        source = x_ref.at[
            plane // 2,
            pl.ds(pl.multiple_of(lax.rem(plane, 2) * HALF, HALF), HALF),
            pl.ds(yh * lanes_of, lanes_of),
        ]
        copy(source, rows_ref.at[yh])
    copy(left_in, left_ref)
    copy(right_in, right_ref)
    copy(lc_in, lc_ref)
    copy(rc_in, rc_ref)
    for yh in range(YH):
        copies[yh].wait()
        for yl in range(YL):
            for zh in range(ZH):
                at = (yl * ZH + zh) * ZL
                first = rows_ref[yh, :, at * WIDE:(at + 1) * WIDE]
                second = rows_ref[yh, :, (at + 1) * WIDE:(at + 2) * WIDE]
                for c in range(CORE):
                    lanes = slice(c * BLOCK, (c + 1) * BLOCK)
                    rows = slice(c * XROWS + yl * HALF, c * XROWS + (yl + 1) * HALF)
                    sent_ref[yh * ZH + zh, rows, :] = jnp.concatenate(
                        [first[:, lanes], second[:, lanes]], axis=1
                    )
        for zh in range(ZH):
            copy(sent_ref.at[yh * ZH + zh], out_ref.at[turned(core, yh, zh, ZH, X_ORDER)])
    for n, (c_ref, in_ref, to_ref) in enumerate(
        ((lc_ref, left_ref, lout_ref), (rc_ref, right_ref, rout_ref))
    ):
        copies[YH + n].wait()
        copies[YH + 2 + n].wait()
        scale = c_ref[...].astype(jnp.float32)
        for p in range(PAIRS):
            both = []
            for t in (2 * p, 2 * p + 1):
                scaled = in_ref[t].astype(jnp.float32) * scale[:, t:t + 1]
                both.append(scaled.astype(jnp.bfloat16))
            to_ref[p * BLOCK:(p + 1) * BLOCK, :] = jnp.concatenate(both, axis=1)
    for done in copies[YH + 4:]:
        done.wait()


def spread_kernel(
    got_ref, left_ref, r0_ref, ra_ref, rb_ref, rc_ref, p0_ref, pa_ref, pb_ref, pc_ref, sent_ref
):
    plane = lax.axis_index("op").astype(jnp.int32)
    core = lax.axis_index("core").astype(jnp.int32)
    wide = CORE * XROWS
    for ref, d in zip((p0_ref, pa_ref, pb_ref, pc_ref), across(core)):
        to = jnp.bitwise_xor(plane, d)
        for z in range(ZH):
            ref[z * wide:(z + 1) * wide, :] = got_ref[turned(core, to, z, ZH, X_ORDER)]
        for right_ref, e in zip((r0_ref, ra_ref, rb_ref, rc_ref), around(core)):
            rows = pl.ds(pl.multiple_of(ZH * wide + e * RROWS, BLOCK), RROWS)
            ref[rows, :] = right_ref[...]
    for to in range(YH * ZH):
        sent_ref[to] = left_ref[...]


def core_kernel(left_ref, p0_ref, pa_ref, pb_ref, pc_ref, own_ref, give_ref, near_ref):
    x_at, _, yl_at, _, zl_at, core = place()
    for ref, d in zip((p0_ref, pa_ref, pb_ref, pc_ref), across(core)):
        x = jnp.bitwise_xor(x_at, d)
        for z in range(ZH):
            rows = slice(z * XROWS, (z + 1) * XROWS)
            for to_ref, c in ((own_ref, core), (give_ref, 1 - core)):
                at = pl.multiple_of((z * CORE + c) * XROWS, XROWS)
                to_ref[x, rows, :] = ref[pl.ds(at, XROWS), :]
        rows = pl.ds(pl.multiple_of(x * RROWS, BLOCK), RROWS)
        for e in range(YL * ZL):
            at = FROM * XROWS + e * RROWS
            near_ref[jnp.bitwise_xor(yl_at * ZL + zl_at, e), rows, :] = ref[at:at + RROWS, :]
    for x in range(XDIM):
        for z in range(ZH):
            rows = slice(ZH * XROWS + z * RROWS, ZH * XROWS + (z + 1) * RROWS)
            left = left_ref[turned(core, x ^ 2, z, ZH, L_ORDER)]
            own_ref[x, rows, :] = left
            give_ref[x, rows, :] = left


def build_right(near_ref, right_ref):
    zeros = jnp.zeros((BLOCK, WIDE), jnp.bfloat16)
    for b in range(4):
        rows = slice(b * BLOCK, (b + 1) * BLOCK)
        used = slice((b // 2) * WIDE, (b // 2 + 1) * WIDE)
        unused = slice((1 - b // 2) * WIDE, (2 - b // 2) * WIDE)
        for d in range(XDIM):
            first = d * HERE
            for p in range(PAIRS):
                at = d * RROWS + p * BLOCK
                piece = near_ref[b, at:at + BLOCK, :]
                for s in range(2):
                    right_ref[first + 2 * p + s, rows, used] = placed(piece, s, b % 2)
                    right_ref[first + 2 * p + s, rows, unused] = zeros


def build_left(got_ref, left_ref):
    zeros = jnp.zeros((BLOCK, WIDE), jnp.bfloat16)
    for x in range(XDIM):
        for z in range(ZH):
            rows = slice(z * BLOCK, (z + 1) * BLOCK)
            for p in range(PAIRS):
                at = ZH * XROWS + z * RROWS + p * BLOCK
                piece = got_ref[x, at:at + BLOCK, :]
                for s in range(2):
                    at = (x * HERE + 2 * p + s) * GROUP
                    used, unused = at + (z // 2) * WIDE, at + (1 - z // 2) * WIDE
                    left_ref[rows, used:used + WIDE] = placed(piece, s, z % 2)
                    left_ref[rows, unused:unused + WIDE] = zeros


def sigma_kernel(c, lcharge_ref, rcharge_ref, got_ref, near_ref, *refs):
    if c == 0:
        out_ref, right_ref, left_ref, half_ref = refs
    else:
        right_ref, _, out_ref, left_ref, half_ref = refs
    x_at, yh_at, yl_at, zh_at, zl_at, core = place()
    if c == 0:
        build_right(near_ref, right_ref)
    vectors = half_ref.shape[0] // GROUP
    for v in range(vectors):
        rows = []
        for z in range(ZH):
            for h in range(2):
                piece = got_ref[v * 2 + h, z * XROWS:(z + 1) * XROWS, :]
                rows.append(jnp.concatenate([piece[:HALF], piece[HALF:]], axis=1))
        state = jnp.concatenate(rows, axis=0)
        for t in range(TERMS):
            out = lax.dot_general(right_ref[t], state, NT, preferred_element_type=jnp.float32)
            half_ref[v * GROUP:(v + 1) * GROUP, t * GROUP:(t + 1) * GROUP] = out.astype(
                half_ref.dtype
            )
    build_left(got_ref, left_ref)
    out = lax.dot_general(half_ref[...], left_ref[...], NT, preferred_element_type=jnp.float32)

    lane = lax.broadcasted_iota(jnp.int32, (1, GROUP), 1) // BLOCK
    charge = jnp.zeros((1, GROUP), jnp.int32)
    for z in range(ZH):
        sector = (((x_at * YL + yl_at) * ZH + z) * ZL + zl_at) * CORE + jnp.bitwise_xor(core, c)
        charge = jnp.where(lane == z, lcharge_ref[sector], charge)
    for b in range(4):
        sector = (((yh_at * YL + b // 2) * ZH + zh_at) * ZL + b % 2) * CORE + core
        allowed = jnp.abs(charge + rcharge_ref[sector] - target_charge) <= 1
        for v in range(vectors):
            at = v * GROUP + b * BLOCK
            block = out[at:at + BLOCK]
            out_ref[turned(core, b // 2, b % 2, ZL, OUT_ORDER), 0, v] = jnp.where(allowed, block, jnp.zeros_like(block)).astype(
                out_ref.dtype
            )


def merge_kernel(in_ref, out_ref):
    core = lax.axis_index("core").astype(jnp.int32)
    for yl in range(YL):
        for zl in range(ZL):
            for m in range(ZH // 2):
                low = in_ref[turned(core, yl, zl, ZL, OUT_ORDER), core, 0, :, m * WIDE:(m + 1) * WIDE]
                high = in_ref[turned(core, yl, zl, ZL, OUT_ORDER), 1 - core, 0, :, m * WIDE:(m + 1) * WIDE]
                for h in range(2):
                    lanes = slice(h * BLOCK, (h + 1) * BLOCK)
                    at = ((yl * ZH + 2 * m + h) * ZL + zl) * WIDE
                    out_ref[0, :, at:at + WIDE] = jnp.concatenate(
                        [low[:, lanes], high[:, lanes]], axis=1
                    )


def exchange(array, ids, axes, order):
    ids = np.moveaxis(ids, [SEC.index(a) for a in axes], [-2, -1])
    at = [a for a in SEC if a not in axes].index("core")
    groups = []
    for index in np.ndindex(*ids.shape[:-2]):
        group = ids[index]
        if index[at] == 1:
            group = group if order == "backwards" else group.T
            group = group if order == "columns" else np.flip(group)
        groups.append([int(n) for n in group.reshape(-1)])
    return lax.all_to_all(array, SEC + ("op",), 0, 0, tiled=True, axis_index_groups=groups)


def partners(axis_of_core, steps):
    pairs = []
    for core in range(CORE):
        for n in range(4):
            to = n ^ steps[core]
            if axis_of_core == 0:
                pairs.append((core * 4 + n, core * 4 + to))
            else:
                pairs.append((n * CORE + core, to * CORE + core))
    return pairs


def body(
    trial_state,
    left_operators,
    right_operators,
    left_coupling,
    right_coupling,
    left_charge,
    right_charge,
):
    vectors, _, states = trial_state.shape
    ids = np.arange(YH * YL * ZH * ZL * CORE * XDIM).reshape(YH, YL, ZH, ZL, CORE, XDIM)
    smem = pl.BlockSpec(memory_space=pltpu.SMEM)
    vmem = pl.BlockSpec(memory_space=pltpu.VMEM)
    anywhere = pl.BlockSpec(memory_space=pl.ANY)
    params = pltpu.CompilerParams(vmem_limit_bytes=VMEM)
    small = pltpu.CompilerParams(vmem_limit_bytes=SMALL)

    wide = CORE * XROWS
    message = jax.ShapeDtypeStruct((YH * ZH, wide, WIDE), jnp.bfloat16)
    operator = jax.ShapeDtypeStruct((RROWS, WIDE), jnp.bfloat16)

    sent, left, right = pl.pallas_call(
        prepare_kernel,
        in_specs=[pl.BlockSpec(memory_space=pltpu.HBM)] * 5,
        out_specs=[anywhere, vmem, vmem],
        out_shape=[message, operator, operator],
        scratch_shapes=[
            pltpu.VMEM((YH * ZH, wide, WIDE), jnp.bfloat16),
            pltpu.VMEM((1, HERE), jnp.int32),
            pltpu.VMEM((1, HERE), jnp.int32),
            pltpu.VMEM(left_operators.shape, jnp.bfloat16),
            pltpu.VMEM(right_operators.shape, jnp.bfloat16),
            pltpu.VMEM((YH, HALF, states // YH), jnp.bfloat16),
            pltpu.SemaphoreType.DMA((YH + 4 + YH * ZH,)),
        ],
        name="prepare_parts",
    )(
        left_coupling.reshape(1, HERE),
        right_coupling.reshape(1, HERE),
        left_operators,
        right_operators,
        trial_state,
    )
    got = exchange(sent, ids, FAR, X_ORDER)

    swap = [(q * XDIM + x, (x ^ 2) * XDIM + q) for q in range(YH) for x in range(XDIM)]
    left = lax.ppermute(left, ("yh", "op"), swap)

    rights = [right] + [
        lax.ppermute(right, NEAR + ("core",), partners(1, [around(c)[n] for c in range(CORE)]))
        for n in (1, 2, 3)
    ]

    pack = jax.ShapeDtypeStruct((ZH * wide + YL * ZL * RROWS, WIDE), jnp.bfloat16)
    *packs, left = pl.pallas_call(
        spread_kernel,
        in_specs=[vmem] * 6,
        out_specs=[vmem] * 5,
        out_shape=[pack] * XDIM + [jax.ShapeDtypeStruct((YH * ZH, RROWS, WIDE), jnp.bfloat16)],
        compiler_params=small,
        name="spread_parts",
    )(got, left, *rights)
    left = exchange(left, ids, FAR, L_ORDER)
    packs = packs[:1] + [
        lax.ppermute(packs[n], ("core", "op"), partners(0, [across(c)[n] for c in range(CORE)]))
        for n in (1, 2, 3)
    ]

    mine = jax.ShapeDtypeStruct((XDIM, ZH * (XROWS + RROWS), WIDE), jnp.bfloat16)
    near = jax.ShapeDtypeStruct((YL * ZL, XDIM * RROWS, WIDE), jnp.bfloat16)
    own, give, right = pl.pallas_call(
        core_kernel,
        in_specs=[vmem] * 5,
        out_specs=[vmem] * 3,
        out_shape=[mine, mine, near],
        compiler_params=small,
        name="sort_cores",
    )(left, *packs)
    other = lax.ppermute(give, "core", [(0, 1), (1, 0)])

    shared = [
        jax.ShapeDtypeStruct((TERMS, GROUP, GROUP), jnp.bfloat16),
        jax.ShapeDtypeStruct((4, CORE, vectors, BLOCK, GROUP), jnp.bfloat16),
    ]
    blocks = [
        pl.BlockSpec((4, 1, vectors, BLOCK, GROUP), lambda i, c=c: (0, c, 0, 0, 0))
        for c in range(CORE)
    ]
    keep = pl.BlockSpec(shared[0].shape, lambda v: (0, 0, 0))
    scratch = [
        pltpu.VMEM((GROUP, TERMS * GROUP), jnp.bfloat16),
        pltpu.VMEM((vectors * GROUP, TERMS * GROUP), jnp.bfloat16),
    ]
    inputs = [smem, smem] + [
        pl.BlockSpec(shape.shape, lambda v: (0, 0, 0)) for shape in (mine, near)
    ]
    partial, diagonal = pl.pallas_call(
        lambda *refs: sigma_kernel(0, *refs),
        grid=(1,),
        in_specs=inputs,
        out_specs=[blocks[0], keep],
        out_shape=shared[::-1],
        scratch_shapes=scratch,
        compiler_params=params,
        name="sigma_own",
    )(left_charge, right_charge, own, right)
    partial = pl.pallas_call(
        lambda lc, rc, got, *refs: sigma_kernel(1, lc, rc, got, None, *refs),
        grid=(1,),
        in_specs=inputs[:3] + [keep, anywhere],
        out_specs=blocks[1],
        out_shape=shared[1],
        scratch_shapes=scratch,
        input_output_aliases={4: 0},
        compiler_params=params,
        name="sigma_other",
    )(left_charge, right_charge, other, diagonal, partial)

    partial = exchange(partial, ids, NEAR, OUT_ORDER)
    return pl.pallas_call(
        merge_kernel,
        grid=(vectors,),
        in_specs=[pl.BlockSpec((4, CORE, 1, BLOCK, GROUP), lambda v: (0, 0, v, 0, 0))],
        out_specs=pl.BlockSpec((1, BLOCK, 8 * GROUP), lambda v: (v, 0, 0)),
        out_shape=jax.ShapeDtypeStruct((vectors, BLOCK, 8 * GROUP), jnp.bfloat16),
        compiler_params=small,
        name="merge_sectors",
    )(partial)


def solution(mesh):
    fine = Mesh(mesh.devices.reshape(YH, YL, ZH, ZL, CORE, XDIM), SEC + ("op",))
    return jax.shard_map(
        body,
        mesh=fine,
        in_specs=(
            P(None, SEC, None),
            P("op", SEC, None),
            P("op", SEC, None),
            P("op", SEC),
            P("op", SEC),
            P(),
            P(),
        ),
        out_specs=P(None, SEC, "op"),
        check_vma=False,
    )
```

```python
import jax
import jax.numpy as jnp
import numpy as np
from jax import lax
from jax.experimental import pallas as pl
from jax.experimental.pallas import tpu as pltpu
from jax.sharding import Mesh, PartitionSpec as P

target_charge = 6
XDIM, YH, YL, ZH, ZL, CORE = 4, 4, 2, 4, 2, 2
SEC = ("yh", "yl", "zh", "zl", "core")
FAR = ("yh", "zh")
NEAR = ("yl", "zl")
X_ORDER, L_ORDER, OUT_ORDER = "backwards", "both", "backwards"
NT = (((1,), (1,)), ((), ()))
BLOCK = 64
WIDE = 2 * BLOCK
HALF = BLOCK // 2
GROUP = 4 * BLOCK
TERMS = 24
HERE = TERMS // XDIM
PAIRS = HERE // 2
XROWS = 2 * HALF
RROWS = PAIRS * BLOCK
FROM = ZH * CORE
VMEM = 24 * 1024 * 1024
SMALL = 8 * 1024 * 1024


def swap_halves(piece):
    return jnp.concatenate([piece[:, BLOCK:], piece[:, :BLOCK]], axis=1)


def placed(piece, second, to_second):
    lane = lax.broadcasted_iota(jnp.int32, piece.shape, 1)
    moved = piece if second == to_second else swap_halves(piece)
    keep = (lane >= BLOCK) if to_second else (lane < BLOCK)
    return jnp.where(keep, moved, jnp.zeros_like(moved))


def across(core):
    return 0, 1 + 2 * core, 2, 3 - 2 * core


def around(core):
    return 0, 1 + core, 2 - core, 3


def place():
    return [lax.axis_index(n).astype(jnp.int32) for n in ("op",) + SEC]


def turned(core, first, second, size, order):
    n, turn = first * size + second, second * size + first
    last = size * size - 1
    return jnp.where(core == 0, n, {"columns": turn, "backwards": last - n, "both": last - turn}[order])


def prepare_kernel(
    lc_in, rc_in, left_in, right_in, x_ref, out_ref, lout_ref, rout_ref,
    sent_ref, lc_ref, rc_ref, left_ref, right_ref, rows_ref, sems,
):
    plane = lax.axis_index("op").astype(jnp.int32)
    core = lax.axis_index("core").astype(jnp.int32)
    lanes_of = rows_ref.shape[2]
    copies = []

    def copy(source, to):
        copies.append(pltpu.make_async_copy(source, to, sems.at[len(copies)]))
        copies[-1].start()

    for yh in range(YH):
        source = x_ref.at[
            plane // 2,
            pl.ds(pl.multiple_of(lax.rem(plane, 2) * HALF, HALF), HALF),
            pl.ds(yh * lanes_of, lanes_of),
        ]
        copy(source, rows_ref.at[yh])
    copy(left_in, left_ref)
    copy(right_in, right_ref)
    copy(lc_in, lc_ref)
    copy(rc_in, rc_ref)
    for yh in range(YH):
        copies[yh].wait()
        for yl in range(YL):
            for zh in range(ZH):
                at = (yl * ZH + zh) * ZL
                first = rows_ref[yh, :, at * WIDE:(at + 1) * WIDE]
                second = rows_ref[yh, :, (at + 1) * WIDE:(at + 2) * WIDE]
                for c in range(CORE):
                    lanes = slice(c * BLOCK, (c + 1) * BLOCK)
                    rows = slice(c * XROWS + yl * HALF, c * XROWS + (yl + 1) * HALF)
                    sent_ref[yh * ZH + zh, rows, :] = jnp.concatenate(
                        [first[:, lanes], second[:, lanes]], axis=1
                    )
        for zh in range(ZH):
            copy(sent_ref.at[yh * ZH + zh], out_ref.at[turned(core, yh, zh, ZH, X_ORDER)])
    for n, (c_ref, in_ref, to_ref) in enumerate(
        ((lc_ref, left_ref, lout_ref), (rc_ref, right_ref, rout_ref))
    ):
        copies[YH + n].wait()
        copies[YH + 2 + n].wait()
        scale = c_ref[...].astype(jnp.float32)
        for p in range(PAIRS):
            both = []
            for t in (2 * p, 2 * p + 1):
                scaled = in_ref[t].astype(jnp.float32) * scale[:, t:t + 1]
                both.append(scaled.astype(jnp.bfloat16))
            to_ref[p * BLOCK:(p + 1) * BLOCK, :] = jnp.concatenate(both, axis=1)
    for done in copies[YH + 4:]:
        done.wait()


def stage_kernel(left_ref, right_ref, sent_ref, own_ref):
    for to in range(YH * ZH):
        sent_ref[to] = left_ref[...]
    own_ref[...] = right_ref[...]


def spread_kernel(
    got_ref, left_ref, r0_ref, ra_ref, rb_ref, rc_ref, p0_ref, pa_ref, pb_ref, pc_ref, sent_ref
):
    plane = lax.axis_index("op").astype(jnp.int32)
    core = lax.axis_index("core").astype(jnp.int32)
    wide = CORE * XROWS
    for ref, d in zip((p0_ref, pa_ref, pb_ref, pc_ref), across(core)):
        to = jnp.bitwise_xor(plane, d)
        for z in range(ZH):
            ref[z * wide:(z + 1) * wide, :] = got_ref[turned(core, to, z, ZH, X_ORDER)]
        for right_ref, e in zip((r0_ref, ra_ref, rb_ref, rc_ref), around(core)):
            rows = pl.ds(pl.multiple_of(ZH * wide + e * RROWS, BLOCK), RROWS)
            ref[rows, :] = right_ref[...]


def core_kernel(left_ref, p0_ref, pa_ref, pb_ref, pc_ref, own_ref, give_ref, near_ref):
    x_at, _, yl_at, _, zl_at, core = place()
    for ref, d in zip((p0_ref, pa_ref, pb_ref, pc_ref), across(core)):
        x = jnp.bitwise_xor(x_at, d)
        for z in range(ZH):
            rows = slice(z * XROWS, (z + 1) * XROWS)
            for to_ref, c in ((own_ref, core), (give_ref, 1 - core)):
                at = pl.multiple_of((z * CORE + c) * XROWS, XROWS)
                to_ref[x, rows, :] = ref[pl.ds(at, XROWS), :]
        rows = pl.ds(pl.multiple_of(x * RROWS, BLOCK), RROWS)
        for e in range(YL * ZL):
            at = FROM * XROWS + e * RROWS
            near_ref[jnp.bitwise_xor(yl_at * ZL + zl_at, e), rows, :] = ref[at:at + RROWS, :]
    for x in range(XDIM):
        for z in range(ZH):
            rows = slice(ZH * XROWS + z * RROWS, ZH * XROWS + (z + 1) * RROWS)
            left = left_ref[turned(core, x ^ 2, z, ZH, L_ORDER)]
            own_ref[x, rows, :] = left
            give_ref[x, rows, :] = left


def build_right(near_ref, right_ref):
    zeros = jnp.zeros((BLOCK, WIDE), jnp.bfloat16)
    for b in range(4):
        rows = slice(b * BLOCK, (b + 1) * BLOCK)
        used = slice((b // 2) * WIDE, (b // 2 + 1) * WIDE)
        unused = slice((1 - b // 2) * WIDE, (2 - b // 2) * WIDE)
        for d in range(XDIM):
            first = d * HERE
            for p in range(PAIRS):
                at = d * RROWS + p * BLOCK
                piece = near_ref[b, at:at + BLOCK, :]
                for s in range(2):
                    right_ref[first + 2 * p + s, rows, used] = placed(piece, s, b % 2)
                    right_ref[first + 2 * p + s, rows, unused] = zeros


def build_left(got_ref, left_ref):
    zeros = jnp.zeros((BLOCK, WIDE), jnp.bfloat16)
    for x in range(XDIM):
        for z in range(ZH):
            rows = slice(z * BLOCK, (z + 1) * BLOCK)
            for p in range(PAIRS):
                at = ZH * XROWS + z * RROWS + p * BLOCK
                piece = got_ref[x, at:at + BLOCK, :]
                for s in range(2):
                    at = (x * HERE + 2 * p + s) * GROUP
                    used, unused = at + (z // 2) * WIDE, at + (1 - z // 2) * WIDE
                    left_ref[rows, used:used + WIDE] = placed(piece, s, z % 2)
                    left_ref[rows, unused:unused + WIDE] = zeros


def sigma_kernel(c, lcharge_ref, rcharge_ref, got_ref, near_ref, *refs):
    if c == 0:
        out_ref, right_ref, left_ref, half_ref = refs
    else:
        right_ref, _, out_ref, left_ref, half_ref = refs
    x_at, yh_at, yl_at, zh_at, zl_at, core = place()
    if c == 0:
        build_right(near_ref, right_ref)
    vectors = half_ref.shape[0] // GROUP
    for v in range(vectors):
        rows = []
        for z in range(ZH):
            for h in range(2):
                piece = got_ref[v * 2 + h, z * XROWS:(z + 1) * XROWS, :]
                rows.append(jnp.concatenate([piece[:HALF], piece[HALF:]], axis=1))
        state = jnp.concatenate(rows, axis=0)
        for t in range(TERMS):
            out = lax.dot_general(right_ref[t], state, NT, preferred_element_type=jnp.float32)
            half_ref[v * GROUP:(v + 1) * GROUP, t * GROUP:(t + 1) * GROUP] = out.astype(
                half_ref.dtype
            )
    build_left(got_ref, left_ref)
    out = lax.dot_general(half_ref[...], left_ref[...], NT, preferred_element_type=jnp.float32)

    lane = lax.broadcasted_iota(jnp.int32, (1, GROUP), 1) // BLOCK
    charge = jnp.zeros((1, GROUP), jnp.int32)
    for z in range(ZH):
        sector = (((x_at * YL + yl_at) * ZH + z) * ZL + zl_at) * CORE + jnp.bitwise_xor(core, c)
        charge = jnp.where(lane == z, lcharge_ref[sector], charge)
    for b in range(4):
        sector = (((yh_at * YL + b // 2) * ZH + zh_at) * ZL + b % 2) * CORE + core
        allowed = jnp.abs(charge + rcharge_ref[sector] - target_charge) <= 1
        for v in range(vectors):
            at = v * GROUP + b * BLOCK
            block = out[at:at + BLOCK]
            out_ref[turned(core, b // 2, b % 2, ZL, OUT_ORDER), 0, v] = jnp.where(allowed, block, jnp.zeros_like(block)).astype(
                out_ref.dtype
            )


def merge_kernel(in_ref, out_ref):
    core = lax.axis_index("core").astype(jnp.int32)
    for yl in range(YL):
        for zl in range(ZL):
            for m in range(ZH // 2):
                low = in_ref[turned(core, yl, zl, ZL, OUT_ORDER), core, 0, :, m * WIDE:(m + 1) * WIDE]
                high = in_ref[turned(core, yl, zl, ZL, OUT_ORDER), 1 - core, 0, :, m * WIDE:(m + 1) * WIDE]
                for h in range(2):
                    lanes = slice(h * BLOCK, (h + 1) * BLOCK)
                    at = ((yl * ZH + 2 * m + h) * ZL + zl) * WIDE
                    out_ref[0, :, at:at + WIDE] = jnp.concatenate(
                        [low[:, lanes], high[:, lanes]], axis=1
                    )


def exchange(array, ids, axes, order):
    ids = np.moveaxis(ids, [SEC.index(a) for a in axes], [-2, -1])
    at = [a for a in SEC if a not in axes].index("core")
    groups = []
    for index in np.ndindex(*ids.shape[:-2]):
        group = ids[index]
        if index[at] == 1:
            group = group if order == "backwards" else group.T
            group = group if order == "columns" else np.flip(group)
        groups.append([int(n) for n in group.reshape(-1)])
    return lax.all_to_all(array, SEC + ("op",), 0, 0, tiled=True, axis_index_groups=groups)


def partners(axis_of_core, steps):
    pairs = []
    for core in range(CORE):
        for n in range(4):
            to = n ^ steps[core]
            if axis_of_core == 0:
                pairs.append((core * 4 + n, core * 4 + to))
            else:
                pairs.append((n * CORE + core, to * CORE + core))
    return pairs


def body(
    trial_state,
    left_operators,
    right_operators,
    left_coupling,
    right_coupling,
    left_charge,
    right_charge,
):
    vectors, _, states = trial_state.shape
    ids = np.arange(YH * YL * ZH * ZL * CORE * XDIM).reshape(YH, YL, ZH, ZL, CORE, XDIM)
    smem = pl.BlockSpec(memory_space=pltpu.SMEM)
    vmem = pl.BlockSpec(memory_space=pltpu.VMEM)
    anywhere = pl.BlockSpec(memory_space=pl.ANY)
    params = pltpu.CompilerParams(vmem_limit_bytes=VMEM)
    small = pltpu.CompilerParams(vmem_limit_bytes=SMALL)

    wide = CORE * XROWS
    message = jax.ShapeDtypeStruct((YH * ZH, wide, WIDE), jnp.bfloat16)
    operator = jax.ShapeDtypeStruct((RROWS, WIDE), jnp.bfloat16)

    sent, left, right = pl.pallas_call(
        prepare_kernel,
        in_specs=[pl.BlockSpec(memory_space=pltpu.HBM)] * 5,
        out_specs=[anywhere, vmem, vmem],
        out_shape=[message, operator, operator],
        scratch_shapes=[
            pltpu.VMEM((YH * ZH, wide, WIDE), jnp.bfloat16),
            pltpu.VMEM((1, HERE), jnp.int32),
            pltpu.VMEM((1, HERE), jnp.int32),
            pltpu.VMEM(left_operators.shape, jnp.bfloat16),
            pltpu.VMEM(right_operators.shape, jnp.bfloat16),
            pltpu.VMEM((YH, HALF, states // YH), jnp.bfloat16),
            pltpu.SemaphoreType.DMA((YH + 4 + YH * ZH,)),
        ],
        name="prepare_parts",
    )(
        left_coupling.reshape(1, HERE),
        right_coupling.reshape(1, HERE),
        left_operators,
        right_operators,
        trial_state,
    )
    got = exchange(sent, ids, FAR, X_ORDER)

    swap = [(q * XDIM + x, (x ^ 2) * XDIM + q) for q in range(YH) for x in range(XDIM)]
    left = lax.ppermute(left, ("yh", "op"), swap)

    rights = [right] + [
        lax.ppermute(right, NEAR + ("core",), partners(1, [around(c)[n] for c in range(CORE)]))
        for n in (1, 2, 3)
    ]

    copies = jax.ShapeDtypeStruct((YH * ZH, RROWS, WIDE), jnp.bfloat16)
    left, rights[0] = pl.pallas_call(
        stage_kernel,
        in_specs=[vmem] * 2,
        out_specs=[vmem] * 2,
        out_shape=[copies, operator],
        compiler_params=small,
        name="stage_parts",
    )(left, right)

    pack = jax.ShapeDtypeStruct((ZH * wide + YL * ZL * RROWS, WIDE), jnp.bfloat16)
    *packs, left = pl.pallas_call(
        spread_kernel,
        in_specs=[vmem, anywhere] + [vmem] * 4,
        out_specs=[vmem] * 4 + [anywhere],
        out_shape=[pack] * XDIM + [copies],
        input_output_aliases={1: XDIM},
        compiler_params=small,
        name="spread_parts",
    )(got, left, *rights)
    left = exchange(left, ids, FAR, L_ORDER)
    packs = packs[:1] + [
        lax.ppermute(packs[n], ("core", "op"), partners(0, [across(c)[n] for c in range(CORE)]))
        for n in (1, 2, 3)
    ]

    mine = jax.ShapeDtypeStruct((XDIM, ZH * (XROWS + RROWS), WIDE), jnp.bfloat16)
    near = jax.ShapeDtypeStruct((YL * ZL, XDIM * RROWS, WIDE), jnp.bfloat16)
    own, give, right = pl.pallas_call(
        core_kernel,
        in_specs=[vmem] * 5,
        out_specs=[vmem] * 3,
        out_shape=[mine, mine, near],
        compiler_params=small,
        name="sort_cores",
    )(left, *packs)
    other = lax.ppermute(give, "core", [(0, 1), (1, 0)])

    shared = [
        jax.ShapeDtypeStruct((TERMS, GROUP, GROUP), jnp.bfloat16),
        jax.ShapeDtypeStruct((4, CORE, vectors, BLOCK, GROUP), jnp.bfloat16),
    ]
    blocks = [
        pl.BlockSpec((4, 1, vectors, BLOCK, GROUP), lambda i, c=c: (0, c, 0, 0, 0))
        for c in range(CORE)
    ]
    keep = pl.BlockSpec(shared[0].shape, lambda v: (0, 0, 0))
    scratch = [
        pltpu.VMEM((GROUP, TERMS * GROUP), jnp.bfloat16),
        pltpu.VMEM((vectors * GROUP, TERMS * GROUP), jnp.bfloat16),
    ]
    inputs = [smem, smem] + [
        pl.BlockSpec(shape.shape, lambda v: (0, 0, 0)) for shape in (mine, near)
    ]
    partial, diagonal = pl.pallas_call(
        lambda *refs: sigma_kernel(0, *refs),
        grid=(1,),
        in_specs=inputs,
        out_specs=[blocks[0], keep],
        out_shape=shared[::-1],
        scratch_shapes=scratch,
        compiler_params=params,
        name="sigma_own",
    )(left_charge, right_charge, own, right)
    partial = pl.pallas_call(
        lambda lc, rc, got, *refs: sigma_kernel(1, lc, rc, got, None, *refs),
        grid=(1,),
        in_specs=inputs[:3] + [keep, anywhere],
        out_specs=blocks[1],
        out_shape=shared[1],
        scratch_shapes=scratch,
        input_output_aliases={4: 0},
        compiler_params=params,
        name="sigma_other",
    )(left_charge, right_charge, other, diagonal, partial)

    partial = exchange(partial, ids, NEAR, OUT_ORDER)
    return pl.pallas_call(
        merge_kernel,
        grid=(vectors,),
        in_specs=[pl.BlockSpec((4, CORE, 1, BLOCK, GROUP), lambda v: (0, 0, v, 0, 0))],
        out_specs=pl.BlockSpec((1, BLOCK, 8 * GROUP), lambda v: (v, 0, 0)),
        out_shape=jax.ShapeDtypeStruct((vectors, BLOCK, 8 * GROUP), jnp.bfloat16),
        compiler_params=small,
        name="merge_sectors",
    )(partial)


def solution(mesh):
    fine = Mesh(mesh.devices.reshape(YH, YL, ZH, ZL, CORE, XDIM), SEC + ("op",))
    return jax.shard_map(
        body,
        mesh=fine,
        in_specs=(
            P(None, SEC, None),
            P("op", SEC, None),
            P("op", SEC, None),
            P("op", SEC),
            P("op", SEC),
            P(),
            P(),
        ),
        out_specs=P(None, SEC, "op"),
        check_vma=False,
    )
```

```python
import jax
import jax.numpy as jnp
import numpy as np
from jax import lax
from jax.experimental import pallas as pl
from jax.experimental.pallas import tpu as pltpu
from jax.sharding import Mesh, PartitionSpec as P

target_charge = 6
XDIM, YH, YL, ZH, ZL, CORE = 4, 4, 2, 4, 2, 2
SEC = ("yh", "yl", "zh", "zl", "core")
FAR = ("yh", "zh")
NEAR = ("yl", "zl")
X_ORDER, L_ORDER, OUT_ORDER = "backwards", "both", "backwards"
NT = (((1,), (1,)), ((), ()))
BLOCK = 64
WIDE = 2 * BLOCK
HALF = BLOCK // 2
GROUP = 4 * BLOCK
TERMS = 24
HERE = TERMS // XDIM
PAIRS = HERE // 2
XROWS = 2 * HALF
RROWS = PAIRS * BLOCK
FROM = ZH * CORE
VMEM = 24 * 1024 * 1024
SMALL = 8 * 1024 * 1024


def swap_halves(piece):
    return jnp.concatenate([piece[:, BLOCK:], piece[:, :BLOCK]], axis=1)


def placed(piece, second, to_second):
    lane = lax.broadcasted_iota(jnp.int32, piece.shape, 1)
    moved = piece if second == to_second else swap_halves(piece)
    keep = (lane >= BLOCK) if to_second else (lane < BLOCK)
    return jnp.where(keep, moved, jnp.zeros_like(moved))


def across(core):
    return 0, 1 + core, 2 + core, 3 - 2 * core


def around(core):
    return 0, 1 + core, 2 - core, 3


def place():
    return [lax.axis_index(n).astype(jnp.int32) for n in ("op",) + SEC]


def turned(core, first, second, size, order):
    n, turn = first * size + second, second * size + first
    last = size * size - 1
    return jnp.where(core == 0, n, {"columns": turn, "backwards": last - n, "both": last - turn}[order])


def prepare_kernel(
    lc_in, rc_in, left_in, right_in, x_ref, out_ref, lout_ref, rout_ref,
    sent_ref, lc_ref, rc_ref, left_ref, right_ref, rows_ref, sems,
):
    plane = lax.axis_index("op").astype(jnp.int32)
    core = lax.axis_index("core").astype(jnp.int32)
    lanes_of = rows_ref.shape[2]
    copies = []

    def copy(source, to):
        copies.append(pltpu.make_async_copy(source, to, sems.at[len(copies)]))
        copies[-1].start()

    for yh in range(YH):
        source = x_ref.at[
            plane // 2,
            pl.ds(pl.multiple_of(lax.rem(plane, 2) * HALF, HALF), HALF),
            pl.ds(yh * lanes_of, lanes_of),
        ]
        copy(source, rows_ref.at[yh])
    copy(left_in, left_ref)
    copy(right_in, right_ref)
    copy(lc_in, lc_ref)
    copy(rc_in, rc_ref)
    for yh in range(YH):
        copies[yh].wait()
        for yl in range(YL):
            for zh in range(ZH):
                at = (yl * ZH + zh) * ZL
                first = rows_ref[yh, :, at * WIDE:(at + 1) * WIDE]
                second = rows_ref[yh, :, (at + 1) * WIDE:(at + 2) * WIDE]
                for c in range(CORE):
                    lanes = slice(c * BLOCK, (c + 1) * BLOCK)
                    rows = slice(c * XROWS + yl * HALF, c * XROWS + (yl + 1) * HALF)
                    sent_ref[yh * ZH + zh, rows, :] = jnp.concatenate(
                        [first[:, lanes], second[:, lanes]], axis=1
                    )
        for zh in range(ZH):
            copy(sent_ref.at[yh * ZH + zh], out_ref.at[turned(core, yh, zh, ZH, X_ORDER)])
    for n, (c_ref, in_ref, to_ref) in enumerate(
        ((lc_ref, left_ref, lout_ref), (rc_ref, right_ref, rout_ref))
    ):
        copies[YH + n].wait()
        copies[YH + 2 + n].wait()
        scale = c_ref[...].astype(jnp.float32)
        for p in range(PAIRS):
            both = []
            for t in (2 * p, 2 * p + 1):
                scaled = in_ref[t].astype(jnp.float32) * scale[:, t:t + 1]
                both.append(scaled.astype(jnp.bfloat16))
            to_ref[p * BLOCK:(p + 1) * BLOCK, :] = jnp.concatenate(both, axis=1)
    for done in copies[YH + 4:]:
        done.wait()


def spread_kernel(
    got_ref, left_ref, r0_ref, ra_ref, rb_ref, rc_ref, p0_ref, pa_ref, pb_ref, pc_ref, sent_ref
):
    plane = lax.axis_index("op").astype(jnp.int32)
    core = lax.axis_index("core").astype(jnp.int32)
    wide = CORE * XROWS
    for ref, d in zip((p0_ref, pa_ref, pb_ref, pc_ref), across(core)):
        to = jnp.bitwise_xor(plane, d)
        for z in range(ZH):
            ref[z * wide:(z + 1) * wide, :] = got_ref[turned(core, to, z, ZH, X_ORDER)]
        for right_ref, e in zip((r0_ref, ra_ref, rb_ref, rc_ref), around(core)):
            rows = pl.ds(pl.multiple_of(ZH * wide + e * RROWS, BLOCK), RROWS)
            ref[rows, :] = right_ref[...]
    for to in range(YH * ZH):
        sent_ref[to] = left_ref[...]


def core_kernel(left_ref, p0_ref, pa_ref, pb_ref, pc_ref, own_ref, give_ref, near_ref):
    x_at, _, yl_at, _, zl_at, core = place()
    for ref, d in zip((p0_ref, pa_ref, pb_ref, pc_ref), across(core)):
        x = jnp.bitwise_xor(x_at, d)
        for z in range(ZH):
            rows = slice(z * XROWS, (z + 1) * XROWS)
            for to_ref, c in ((own_ref, core), (give_ref, 1 - core)):
                at = pl.multiple_of((z * CORE + c) * XROWS, XROWS)
                to_ref[x, rows, :] = ref[pl.ds(at, XROWS), :]
        rows = pl.ds(pl.multiple_of(x * RROWS, BLOCK), RROWS)
        for e in range(YL * ZL):
            at = FROM * XROWS + e * RROWS
            near_ref[jnp.bitwise_xor(yl_at * ZL + zl_at, e), rows, :] = ref[at:at + RROWS, :]
    for x in range(XDIM):
        for z in range(ZH):
            rows = slice(ZH * XROWS + z * RROWS, ZH * XROWS + (z + 1) * RROWS)
            left = left_ref[turned(core, x ^ 2, z, ZH, L_ORDER)]
            own_ref[x, rows, :] = left
            give_ref[x, rows, :] = left


def build_right(near_ref, right_ref):
    zeros = jnp.zeros((BLOCK, WIDE), jnp.bfloat16)
    for b in range(4):
        rows = slice(b * BLOCK, (b + 1) * BLOCK)
        used = slice((b // 2) * WIDE, (b // 2 + 1) * WIDE)
        unused = slice((1 - b // 2) * WIDE, (2 - b // 2) * WIDE)
        for d in range(XDIM):
            first = d * HERE
            for p in range(PAIRS):
                at = d * RROWS + p * BLOCK
                piece = near_ref[b, at:at + BLOCK, :]
                for s in range(2):
                    right_ref[first + 2 * p + s, rows, used] = placed(piece, s, b % 2)
                    right_ref[first + 2 * p + s, rows, unused] = zeros


def build_left(got_ref, left_ref):
    zeros = jnp.zeros((BLOCK, WIDE), jnp.bfloat16)
    for x in range(XDIM):
        for z in range(ZH):
            rows = slice(z * BLOCK, (z + 1) * BLOCK)
            for p in range(PAIRS):
                at = ZH * XROWS + z * RROWS + p * BLOCK
                piece = got_ref[x, at:at + BLOCK, :]
                for s in range(2):
                    at = (x * HERE + 2 * p + s) * GROUP
                    used, unused = at + (z // 2) * WIDE, at + (1 - z // 2) * WIDE
                    left_ref[rows, used:used + WIDE] = placed(piece, s, z % 2)
                    left_ref[rows, unused:unused + WIDE] = zeros


def sigma_kernel(c, lcharge_ref, rcharge_ref, got_ref, near_ref, *refs):
    if c == 0:
        out_ref, right_ref, left_ref, half_ref = refs
    else:
        right_ref, _, out_ref, left_ref, half_ref = refs
    x_at, yh_at, yl_at, zh_at, zl_at, core = place()
    if c == 0:
        build_right(near_ref, right_ref)
    vectors = half_ref.shape[0] // GROUP
    for v in range(vectors):
        rows = []
        for z in range(ZH):
            for h in range(2):
                piece = got_ref[v * 2 + h, z * XROWS:(z + 1) * XROWS, :]
                rows.append(jnp.concatenate([piece[:HALF], piece[HALF:]], axis=1))
        state = jnp.concatenate(rows, axis=0)
        for t in range(TERMS):
            out = lax.dot_general(right_ref[t], state, NT, preferred_element_type=jnp.float32)
            half_ref[v * GROUP:(v + 1) * GROUP, t * GROUP:(t + 1) * GROUP] = out.astype(
                half_ref.dtype
            )
    build_left(got_ref, left_ref)
    out = lax.dot_general(half_ref[...], left_ref[...], NT, preferred_element_type=jnp.float32)

    lane = lax.broadcasted_iota(jnp.int32, (1, GROUP), 1) // BLOCK
    charge = jnp.zeros((1, GROUP), jnp.int32)
    for z in range(ZH):
        sector = (((x_at * YL + yl_at) * ZH + z) * ZL + zl_at) * CORE + jnp.bitwise_xor(core, c)
        charge = jnp.where(lane == z, lcharge_ref[sector], charge)
    for b in range(4):
        sector = (((yh_at * YL + b // 2) * ZH + zh_at) * ZL + b % 2) * CORE + core
        allowed = jnp.abs(charge + rcharge_ref[sector] - target_charge) <= 1
        for v in range(vectors):
            at = v * GROUP + b * BLOCK
            block = out[at:at + BLOCK]
            out_ref[turned(core, b // 2, b % 2, ZL, OUT_ORDER), 0, v] = jnp.where(allowed, block, jnp.zeros_like(block)).astype(
                out_ref.dtype
            )


def merge_kernel(in_ref, out_ref):
    core = lax.axis_index("core").astype(jnp.int32)
    for yl in range(YL):
        for zl in range(ZL):
            for m in range(ZH // 2):
                low = in_ref[turned(core, yl, zl, ZL, OUT_ORDER), core, 0, :, m * WIDE:(m + 1) * WIDE]
                high = in_ref[turned(core, yl, zl, ZL, OUT_ORDER), 1 - core, 0, :, m * WIDE:(m + 1) * WIDE]
                for h in range(2):
                    lanes = slice(h * BLOCK, (h + 1) * BLOCK)
                    at = ((yl * ZH + 2 * m + h) * ZL + zl) * WIDE
                    out_ref[0, :, at:at + WIDE] = jnp.concatenate(
                        [low[:, lanes], high[:, lanes]], axis=1
                    )


def exchange(array, ids, axes, order):
    ids = np.moveaxis(ids, [SEC.index(a) for a in axes], [-2, -1])
    at = [a for a in SEC if a not in axes].index("core")
    groups = []
    for index in np.ndindex(*ids.shape[:-2]):
        group = ids[index]
        if index[at] == 1:
            group = group if order == "backwards" else group.T
            group = group if order == "columns" else np.flip(group)
        groups.append([int(n) for n in group.reshape(-1)])
    return lax.all_to_all(array, SEC + ("op",), 0, 0, tiled=True, axis_index_groups=groups)


def partners(axis_of_core, steps):
    pairs = []
    for core in range(CORE):
        for n in range(4):
            to = n ^ steps[core]
            if axis_of_core == 0:
                pairs.append((core * 4 + n, core * 4 + to))
            else:
                pairs.append((n * CORE + core, to * CORE + core))
    return pairs


def body(
    trial_state,
    left_operators,
    right_operators,
    left_coupling,
    right_coupling,
    left_charge,
    right_charge,
):
    vectors, _, states = trial_state.shape
    ids = np.arange(YH * YL * ZH * ZL * CORE * XDIM).reshape(YH, YL, ZH, ZL, CORE, XDIM)
    smem = pl.BlockSpec(memory_space=pltpu.SMEM)
    vmem = pl.BlockSpec(memory_space=pltpu.VMEM)
    anywhere = pl.BlockSpec(memory_space=pl.ANY)
    params = pltpu.CompilerParams(vmem_limit_bytes=VMEM)
    small = pltpu.CompilerParams(vmem_limit_bytes=SMALL)

    wide = CORE * XROWS
    message = jax.ShapeDtypeStruct((YH * ZH, wide, WIDE), jnp.bfloat16)
    operator = jax.ShapeDtypeStruct((RROWS, WIDE), jnp.bfloat16)

    sent, left, right = pl.pallas_call(
        prepare_kernel,
        in_specs=[pl.BlockSpec(memory_space=pltpu.HBM)] * 5,
        out_specs=[anywhere, vmem, vmem],
        out_shape=[message, operator, operator],
        scratch_shapes=[
            pltpu.VMEM((YH * ZH, wide, WIDE), jnp.bfloat16),
            pltpu.VMEM((1, HERE), jnp.int32),
            pltpu.VMEM((1, HERE), jnp.int32),
            pltpu.VMEM(left_operators.shape, jnp.bfloat16),
            pltpu.VMEM(right_operators.shape, jnp.bfloat16),
            pltpu.VMEM((YH, HALF, states // YH), jnp.bfloat16),
            pltpu.SemaphoreType.DMA((YH + 4 + YH * ZH,)),
        ],
        name="prepare_parts",
    )(
        left_coupling.reshape(1, HERE),
        right_coupling.reshape(1, HERE),
        left_operators,
        right_operators,
        trial_state,
    )
    got = exchange(sent, ids, FAR, X_ORDER)

    swap = [(q * XDIM + x, (x ^ 2) * XDIM + q) for q in range(YH) for x in range(XDIM)]
    left = lax.ppermute(left, ("yh", "op"), swap)

    rights = [right] + [
        lax.ppermute(right, NEAR + ("core",), partners(1, [around(c)[n] for c in range(CORE)]))
        for n in (1, 2, 3)
    ]

    pack = jax.ShapeDtypeStruct((ZH * wide + YL * ZL * RROWS, WIDE), jnp.bfloat16)
    *packs, left = pl.pallas_call(
        spread_kernel,
        in_specs=[vmem] * 6,
        out_specs=[vmem] * 5,
        out_shape=[pack] * XDIM + [jax.ShapeDtypeStruct((YH * ZH, RROWS, WIDE), jnp.bfloat16)],
        compiler_params=small,
        name="spread_parts",
    )(got, left, *rights)
    left = exchange(left, ids, FAR, L_ORDER)
    packs = packs[:1] + [
        lax.ppermute(packs[n], ("core", "op"), partners(0, [across(c)[n] for c in range(CORE)]))
        for n in (1, 2, 3)
    ]

    mine = jax.ShapeDtypeStruct((XDIM, ZH * (XROWS + RROWS), WIDE), jnp.bfloat16)
    near = jax.ShapeDtypeStruct((YL * ZL, XDIM * RROWS, WIDE), jnp.bfloat16)
    own, give, right = pl.pallas_call(
        core_kernel,
        in_specs=[vmem] * 5,
        out_specs=[vmem] * 3,
        out_shape=[mine, mine, near],
        compiler_params=small,
        name="sort_cores",
    )(left, *packs)
    other = lax.ppermute(give, "core", [(0, 1), (1, 0)])

    shared = [
        jax.ShapeDtypeStruct((TERMS, GROUP, GROUP), jnp.bfloat16),
        jax.ShapeDtypeStruct((4, CORE, vectors, BLOCK, GROUP), jnp.bfloat16),
    ]
    blocks = [
        pl.BlockSpec((4, 1, vectors, BLOCK, GROUP), lambda i, c=c: (0, c, 0, 0, 0))
        for c in range(CORE)
    ]
    keep = pl.BlockSpec(shared[0].shape, lambda v: (0, 0, 0))
    scratch = [
        pltpu.VMEM((GROUP, TERMS * GROUP), jnp.bfloat16),
        pltpu.VMEM((vectors * GROUP, TERMS * GROUP), jnp.bfloat16),
    ]
    inputs = [smem, smem] + [
        pl.BlockSpec(shape.shape, lambda v: (0, 0, 0)) for shape in (mine, near)
    ]
    partial, diagonal = pl.pallas_call(
        lambda *refs: sigma_kernel(0, *refs),
        grid=(1,),
        in_specs=inputs,
        out_specs=[blocks[0], keep],
        out_shape=shared[::-1],
        scratch_shapes=scratch,
        compiler_params=params,
        name="sigma_own",
    )(left_charge, right_charge, own, right)
    partial = pl.pallas_call(
        lambda lc, rc, got, *refs: sigma_kernel(1, lc, rc, got, None, *refs),
        grid=(1,),
        in_specs=inputs[:3] + [keep, anywhere],
        out_specs=blocks[1],
        out_shape=shared[1],
        scratch_shapes=scratch,
        input_output_aliases={4: 0},
        compiler_params=params,
        name="sigma_other",
    )(left_charge, right_charge, other, diagonal, partial)

    partial = exchange(partial, ids, NEAR, OUT_ORDER)
    return pl.pallas_call(
        merge_kernel,
        grid=(vectors,),
        in_specs=[pl.BlockSpec((4, CORE, 1, BLOCK, GROUP), lambda v: (0, 0, v, 0, 0))],
        out_specs=pl.BlockSpec((1, BLOCK, 8 * GROUP), lambda v: (v, 0, 0)),
        out_shape=jax.ShapeDtypeStruct((vectors, BLOCK, 8 * GROUP), jnp.bfloat16),
        compiler_params=small,
        name="merge_sectors",
    )(partial)


def solution(mesh):
    fine = Mesh(mesh.devices.reshape(YH, YL, ZH, ZL, CORE, XDIM), SEC + ("op",))
    return jax.shard_map(
        body,
        mesh=fine,
        in_specs=(
            P(None, SEC, None),
            P("op", SEC, None),
            P("op", SEC, None),
            P("op", SEC),
            P("op", SEC),
            P(),
            P(),
        ),
        out_specs=P(None, SEC, "op"),
        check_vma=False,
    )
```
